512 devices in a mesh: section: 2 (over x_hi), expert: 16 (over z, core), dp: 16 (over x_lo, y).
Axes of the slice: x: 4 (x_hi: 2, x_lo: 2; x = x_hi * 2 + x_lo), y: 8, z: 8, core: 2. Of those that a mesh axis runs over, the one named last changes fastest.
Arguments:
- tokens: bfloat16 [4096, 3584], P(('section', 'expert', 'dp')), may hold values from -6 to 6
- route_ids: int32 [4096, 2], P(('section', 'expert', 'dp')), may hold values from 0 to 15, as said below
- route_weight: float32 [4096, 2], P(('section', 'expert', 'dp')), may hold values from 0.2 to 2
- gate_weight: bfloat16 [32, 3584, 2048], P(('section', 'expert'), None, 'dp'), may hold values from -0.09375 to 0.09375
- up_weight: bfloat16 [32, 3584, 2048], P(('section', 'expert'), None, 'dp'), may hold values from -0.09375 to 0.09375
- down_weight: bfloat16 [32, 2048, 3584], P(('section', 'expert'), 'dp'), may hold values from -0.125 to 0.125
- latent_cache: bfloat16 [1024, 256, 576], P(('section', 'expert', 'dp')), may hold values from -6 to 6
- cache_len: int32 [1024], replicated, may hold values from 2 to 256
- hand_source: int32 [16, 16], P('expert'), may hold values from 0 to 15, each once within a row
- hand_slot: int32 [16, 16], P('expert'), may hold values from 0 to 1
- query_latent: bfloat16 [1536, 2, 36864], P(('section', 'expert', 'dp')), may hold values from -32 to 32
- new_latent: bfloat16 [1536, 2, 576], P(('section', 'expert', 'dp')), may hold values from -6 to 6
Outputs:
- moe_out: bfloat16 [4096, 3584], P(('section', 'expert', 'dp'))
- attention_out: bfloat16 [1536, 2, 32768], P(('section', 'expert', 'dp'))
The draws below stay inside these ranges and needn't reach their ends.
Inputs may be any that keep to these rules, and one draw needn't show every extreme that they name: `route_ids`: each token names 2 different experts; the 8 tokens of one device name one expert at most 2 times. `hand_source`: each row is a permutation of the dp indices: every prefill device of an expert index hands exactly one request, and every decode device receives exactly one.
All inputs are finite; a program needn't handle non-finite values.
Results may differ from the reference program's by a relative error of at most 0.025.
Values may be sent and summed in bfloat16 or wider, within the bound.
A program may use at most 64 MiB of HBM per device.

```python
import math
import jax
import jax.numpy as jnp
from jax import lax

D = 3584
FF = 2048
EXPERTS = 16
TOPK = 2
CAP = 2
TOK_DEV = 8
HEADS = 64
KVL = 512
LAT = 576
LMAX = 256
REQ_DEV = 2
QSTEP = 2
SLOTS = 3
SEC_TOKENS = 2048
TOKENS = 4096
REQUESTS = 1024
ALL_EXPERTS = 32
N_SECTION = 2
N_EXPERT = 16
N_DP = 16
DEVICES = 512


def draw_latent_cache(key, part):
    key = jax.random.fold_in(key, 7)
    return jax.random.truncated_normal(key, -6.0, 6.0, (REQUESTS, LMAX, LAT), jnp.float32).astype(jnp.bfloat16)


def draw_query_latent(key, part):
    key = jax.random.fold_in(key, 9)
    values = jax.random.truncated_normal(key, -6.0, 6.0, (DEVICES * SLOTS, QSTEP, HEADS * LAT), jnp.float32)
    return values.astype(jnp.bfloat16)


def draw_cache_len(key, part):
    key = jax.random.fold_in(key, 3)
    length_key, place_key = jax.random.split(key)
    lengths = jax.random.randint(length_key, (REQUESTS,), 2, LMAX + 1)
    longest = jax.random.randint(place_key, (), 0, REQUESTS)
    return jnp.where(jnp.arange(REQUESTS) == longest, LMAX, lengths).astype(jnp.int32)


def draw_route_ids(key, part):
    key = jax.random.fold_in(key, 5)
    block_total = TOKENS // TOK_DEV
    per_section = block_total // N_SECTION
    pick_total = TOK_DEV * TOPK
    remaining = pick_total - CAP
    most_full = remaining // CAP
    least_full = max(0, -(-(remaining - (EXPERTS - 1)) // (CAP - 1)))
    hot_key, full_key, block_key = jax.random.split(key, 3)
    hot_expert = jax.random.randint(hot_key, (N_SECTION,), 0, EXPERTS)
    full_count = jax.random.randint(full_key, (block_total,), least_full, most_full + 1)

    def one_block(this_key, hot_one, full_one):
        perm_key, row_key = jax.random.split(this_key)
        others = jax.random.permutation(perm_key, EXPERTS - 1)
        others = others + (others >= hot_one).astype(others.dtype)
        ranking = jnp.arange(EXPERTS - 1)
        singles = remaining - full_one * CAP
        other_counts = jnp.where(ranking < full_one, CAP, jnp.where(ranking < full_one + singles, 1, 0))
        counts = jnp.zeros((EXPERTS,), jnp.int32).at[others].set(other_counts.astype(jnp.int32))
        counts = counts.at[hot_one].set(CAP)
        bounds = jnp.cumsum(counts)
        pick_pos = jnp.arange(pick_total)
        listed = jnp.sum((bounds[None, :] <= pick_pos[:, None]).astype(jnp.int32), axis=1)
        pick_table = listed.reshape(TOPK, TOK_DEV).T
        return pick_table[jax.random.permutation(row_key, TOK_DEV)]
    block_keys = jax.random.split(block_key, block_total)
    hot_blocks = jnp.repeat(hot_expert, per_section)
    drawn = jax.vmap(one_block)(block_keys, hot_blocks, full_count)
    return drawn.reshape(TOKENS, TOPK).astype(jnp.int32)


def with_ends(entries, key, least, top_value):
    dims = entries.shape
    index_at = [jax.random.randint(jax.random.fold_in(key, axis), (), 0, dims[axis]) for axis in range(len(dims))]
    entries = entries.at[tuple(index_at)].set(least)
    longest = dims.index(max(dims))
    index_at[longest] = (index_at[longest] + 1) % dims[longest]
    return entries.at[tuple(index_at)].set(top_value)


def steps_of(rng, dims, shards, low, largest):
    level = 1.0
    for dim, blocks in shards:
        heights = jax.random.uniform(jax.random.fold_in(jax.random.fold_in(rng, 6), dim), (blocks,), jnp.float32, low / len(shards), largest / len(shards))
        level = level * jnp.repeat(jnp.exp(heights), dims[dim] // blocks).reshape((-1,) + (1,) * (len(dims) - 1 - dim))
    return level


def noise(stream_key, shape, width, bound, shards=(), kind=jnp.bfloat16):
    level = steps_of(stream_key, shape, shards, -0.22, 0.18) if shards else 1.0
    values = jax.random.normal(stream_key, shape, jnp.float32) * width * level
    return jnp.minimum(jnp.maximum(values, -bound), bound).astype(kind)


def setup_inputs(seed: int = 0) -> dict:
    arg_keys = jax.random.split(jax.random.key(seed), 13)
    tokens = noise(arg_keys[0], (TOKENS, D), 1.0, 6.0, ((0, 512),))
    route_ids = draw_route_ids(jax.random.fold_in(arg_keys[12], 71), 0)
    route_weight = jnp.clip(jnp.exp(math.log(2.0) - 2.3025851 * jax.random.uniform(arg_keys[2], (TOKENS, TOPK), jnp.float32) ** steps_of(arg_keys[2], (TOKENS, TOPK), ((0, 512),), -0.2, 0.2)), 0.2, 2.0)
    gate_weight = noise(arg_keys[3], (ALL_EXPERTS, D, FF), D ** -0.5, 0.09375, ((0, 32), (2, 16)))
    up_weight = noise(arg_keys[4], (ALL_EXPERTS, D, FF), D ** -0.5, 0.09375, ((0, 32), (2, 16)))
    down_weight = noise(arg_keys[5], (ALL_EXPERTS, FF, D), FF ** -0.5, 0.125, ((0, 32), (1, 16)))
    latent_cache = draw_latent_cache(jax.random.fold_in(arg_keys[12], 71), 0)
    cache_len = draw_cache_len(jax.random.fold_in(arg_keys[12], 71), 0)
    hand_source = jax.vmap(lambda own: jax.random.permutation(own, N_DP))(jax.random.split(arg_keys[8], N_EXPERT)).reshape((N_EXPERT, N_DP)).astype(jnp.int32)
    hand_slot = with_ends(jax.random.randint(arg_keys[9], (N_EXPERT, N_DP), 0, REQ_DEV), jax.random.fold_in(arg_keys[9], 1), 0, REQ_DEV - 1).astype(jnp.int32)
    query_latent = draw_query_latent(jax.random.fold_in(arg_keys[12], 71), 0)
    new_latent = noise(arg_keys[11], (DEVICES * SLOTS, QSTEP, LAT), 1.0, 6.0, ((0, 512),))
    return dict(tokens=tokens, route_ids=route_ids, route_weight=route_weight, gate_weight=gate_weight, up_weight=up_weight, down_weight=down_weight, latent_cache=latent_cache, cache_len=cache_len, hand_source=hand_source, hand_slot=hand_slot, query_latent=query_latent, new_latent=new_latent)


softmax_scale = 192.0 ** -0.5


def expert_outputs(tokens, route_ids, gate_weight, up_weight, down_weight):
    pair_total = TOKENS * TOPK
    pair_token = (jnp.arange(pair_total) // TOPK).astype(jnp.int32)
    section_of = pair_token // SEC_TOKENS
    group_key = (section_of * EXPERTS + route_ids.reshape(-1)).astype(jnp.int32)
    sort_order = jnp.argsort(group_key, stable=True).astype(jnp.int32)
    sorted_key = group_key[sort_order]
    targets = jnp.arange(ALL_EXPERTS, dtype=jnp.int32)
    starts = jnp.searchsorted(sorted_key, targets, side="left").astype(jnp.int32)
    stop_at = jnp.searchsorted(sorted_key, targets, side="right").astype(jnp.int32)
    capacity = N_EXPERT * N_DP * CAP
    padded = jnp.concatenate([sort_order, jnp.zeros((capacity,), jnp.int32)])

    def one_expert(expert_number):
        picked = lax.dynamic_slice(padded, (starts[expert_number],), (capacity,))
        token_rows = tokens[pair_token[picked]]
        gate_proj = jnp.dot(token_rows, gate_weight[expert_number], preferred_element_type=jnp.float32)
        up_proj = jnp.dot(token_rows, up_weight[expert_number], preferred_element_type=jnp.float32)
        hidden = (jax.nn.silu(gate_proj) * up_proj).astype(jnp.bfloat16)
        pieces = hidden.reshape(capacity, N_DP, FF // N_DP).astype(jnp.float32)
        down_rows = down_weight[expert_number].reshape(N_DP, FF // N_DP, D).astype(jnp.float32)
        partial_value = jnp.einsum("rjf,jfd->rjd", pieces, down_rows).astype(jnp.bfloat16)
        result = jnp.sum(partial_value.astype(jnp.float32), axis=1).astype(jnp.bfloat16)
        is_valid = jnp.arange(capacity) < (stop_at[expert_number] - starts[expert_number])
        target = jnp.where(is_valid, picked, pair_total).astype(jnp.int32)
        return result, target

    results, target_rows = lax.map(one_expert, targets)
    placed = jnp.zeros((pair_total, D), jnp.bfloat16)
    placed = placed.at[target_rows.reshape(-1)].set(results.reshape(-1, D), mode="drop")
    return placed.reshape(TOKENS, TOPK, D)


def attend_slot(slot_number, query_latent, new_latent, latent_cache, cache_len, hand_source, hand_slot):
    device = slot_number // SLOTS
    slot_place = slot_number % SLOTS
    section = device // (N_EXPERT * N_DP)
    expert_group = (device // N_DP) % N_EXPERT
    dp_index = device % N_DP
    source = expert_group * N_DP + hand_source[expert_group, dp_index]
    is_own = slot_place < REQ_DEV
    cache_row = jnp.where(is_own, device * REQ_DEV + jnp.minimum(slot_place, REQ_DEV - 1),
                          source * REQ_DEV + hand_slot[expert_group, dp_index]).astype(jnp.int32)
    length = jnp.where(is_own | (section == 1), cache_len[cache_row], 0)
    key_rows = jnp.concatenate([latent_cache[cache_row], new_latent[slot_number]], axis=0).astype(jnp.float32)
    queries = query_latent[slot_number].reshape(QSTEP, HEADS, LAT).astype(jnp.float32)
    scores = softmax_scale * jnp.einsum("qhl,jl->qhj", queries, key_rows)
    position = jnp.arange(LMAX + QSTEP)
    step_ids = jnp.arange(QSTEP)
    visible = jnp.where(position[None, :] < LMAX, position[None, :] < length,
                        position[None, :] - LMAX <= step_ids[:, None])
    scores = jnp.where(visible[:, None, :], scores, -jnp.inf)
    row_max = jnp.max(scores, axis=2, keepdims=True)
    weights = jnp.exp(scores - row_max)
    probability = (weights / jnp.sum(weights, axis=2, keepdims=True)).astype(jnp.bfloat16)
    context = jnp.einsum("qhj,jv->qhv", probability.astype(jnp.float32), key_rows[:, :KVL])
    return context.astype(jnp.bfloat16).reshape(QSTEP, HEADS * KVL)


def reference(tokens, route_ids, route_weight, gate_weight, up_weight, down_weight, latent_cache, cache_len, hand_source, hand_slot, query_latent, new_latent):
    expert_rows = expert_outputs(tokens, route_ids, gate_weight, up_weight, down_weight)
    moe_out = jnp.sum(route_weight[:, :, None] * expert_rows.astype(jnp.float32), axis=1).astype(jnp.bfloat16)

    def attend(slot_number):
        return attend_slot(slot_number, query_latent, new_latent, latent_cache, cache_len, hand_source, hand_slot)

    attention_out = lax.map(attend, jnp.arange(DEVICES * SLOTS, dtype=jnp.int32))
    return moe_out, attention_out
```

```python
import jax
import jax.numpy as jnp
from jax import lax
from jax.experimental import pallas as pl
from jax.experimental.pallas import tpu as pltpu
from jax.sharding import PartitionSpec as P

CAP = 2
ROPE = 64
RING = 8
SPLIT = 1536
MESH = pl.DeviceIdType.MESH

softmax_scale = 192.0 ** (-0.5)
highest = lax.Precision.HIGHEST


def slot(col, way, hops):
    if hops == 0:
        return col
    if hops == 4:
        return 14 + col
    return 2 + (hops - 1) * 4 + col * 2 + way


def add_rows(target, rows, other, other_rows, start, stop, chunk=512):
    def body(i, carry):
        cols = pl.ds(pl.multiple_of(start + i * chunk, chunk), chunk)
        from_cols = pl.ds(pl.multiple_of(i * chunk, chunk), chunk)
        total = target[rows, cols].astype(jnp.float32) + other[other_rows, from_cols].astype(jnp.float32)
        target[rows, cols] = total.astype(jnp.bfloat16)
        return carry

    lax.fori_loop(0, (stop - start) // chunk, body, 0)


def exchange(
    source_ref,
    hand_slot_ref,
    len_ref,
    tokens_ref,
    ids_ref,
    weight_ref,
    new_ref,
    cache_ref,
    query_ref,
    gate_ref,
    up_ref,
    down_ref,
    moe_ref,
    context_ref,
    picked_rows,
    leaving,
    landed,
    rows,
    parts,
    from_y,
    from_y_other,
    from_x,
    from_x_last,
    going,
    coming,
    cache,
    query,
    fresh,
    chosen,
    held,
    pick_pair,
    pick_out,
    picked,
    handed_half,
    handed,
    gate_up,
    down,
    send_sem,
    recv_sem,
    local_sem,
):
    width = rows.shape[1]
    section = lax.axis_index("section")
    expert = lax.axis_index("expert")
    dp = lax.axis_index("dp")
    experts = leaving.shape[0]
    x = dp // RING
    y = lax.rem(dp, RING)
    y_next = {"dp": x * RING + lax.rem(y + 1, RING)}
    y_back = {"dp": x * RING + lax.rem(y + RING - 1, RING)}
    across = {"dp": (1 - x) * RING + y}
    other_section = {"section": 1 - section}
    ways = (y_next, y_back)
    homeward = (y_back, y_next)

    loads = [
        pltpu.make_async_copy(gate_ref, gate_up.at[:, 0:128], local_sem.at[0]),
        pltpu.make_async_copy(up_ref, gate_up.at[:, 128:256], local_sem.at[1]),
        pltpu.make_async_copy(down_ref, down, local_sem.at[2]),
        pltpu.make_async_copy(query_ref, query, local_sem.at[3]),
    ]
    cache_load = pltpu.make_async_copy(cache_ref, cache, local_sem.at[4])
    cache_load.start()
    for load in loads:
        load.start()

    barrier = pltpu.get_barrier_semaphore()
    for peer in (y_next, y_back, across, other_section):
        pl.semaphore_signal(barrier, inc=1, device_id=peer, device_id_type=MESH)
    for j in range(1, experts):
        peer = {"expert": lax.rem(expert + j, experts)}
        pl.semaphore_signal(barrier, inc=1, device_id=peer, device_id_type=MESH)

    choices, tok_rows = ids_ref.shape
    slots = experts * CAP
    relative = lax.rem(ids_ref[...] - expert + experts, experts)
    slot_row = lax.broadcasted_iota(jnp.int32, (slots, tok_rows), 0)
    hits = jnp.zeros((slots, tok_rows), jnp.float32)
    mixing = jnp.zeros((slots, tok_rows), jnp.float32)
    for k in range(choices):
        hit = relative[k : k + 1, :] == slot_row // CAP
        hits = hits + jnp.where(hit, 1.0, 0.0)
        mixing = mixing + jnp.where(hit, weight_ref[k : k + 1, :], 0.0)
    token_row = lax.broadcasted_iota(jnp.int32, (tok_rows, tok_rows), 0)
    token_lane = lax.broadcasted_iota(jnp.int32, (tok_rows, tok_rows), 1)
    before = jnp.where(token_row < token_lane, 1.0, 0.0)
    earlier = jnp.dot(
        hits.astype(jnp.bfloat16), before.astype(jnp.bfloat16), preferred_element_type=jnp.float32
    )
    taken = jnp.where(earlier == lax.rem(slot_row, CAP).astype(jnp.float32), hits, 0.0)
    mixing = mixing * taken
    picked_rows[...] = jnp.dot(
        taken.astype(jnp.bfloat16), tokens_ref[...], preferred_element_type=jnp.float32
    ).astype(jnp.bfloat16)
    for j in range(1, experts):
        leaving[j] = picked_rows[CAP * j : CAP * (j + 1), :]
    pl.semaphore_wait(barrier, 4 + experts - 1)

    count = [0]
    sent = []

    def copy_to(src, dst, device):
        number = count[0]
        count[0] += 1
        return pltpu.make_async_remote_copy(
            src_ref=src,
            dst_ref=dst,
            send_sem=send_sem.at[number],
            recv_sem=recv_sem.at[number],
            device_id=device,
            device_id_type=MESH,
        )

    def send(src, dst, device):
        copy = copy_to(src, dst, device)
        copy.start()
        sent.append(copy)
        return copy

    dispatch = [
        send(leaving.at[j], landed.at[j], {"expert": lax.rem(expert + j, experts)})
        for j in range(1, experts)
    ]

    chosen_slot = 0
    for j in range(2 * RING):
        chosen_slot += jnp.where(source_ref[0, j] == dp, hand_slot_ref[0, j], 0)
    cache_load.wait()
    chosen[...] = cache[chosen_slot]
    half = held.shape[2]
    lat = held.shape[1]
    first_cross = copy_to(chosen.at[:, half : 2 * half], held.at[0], other_section)

    @pl.when(section == 0)
    def _():
        first_cross.start()
        held[0] = chosen[:, 0:half]

    @pl.when(section == 1)
    def _():
        first_cross.wait_recv()

    def hand_hop(hops):
        if hops < 4:
            ahead = send(held.at[(RING - hops + 1) % RING], held.at[RING - hops], y_next)
            back = send(held.at[hops - 1], held.at[hops], y_back)
        else:
            ahead = send(held.at[RING - 3, 0 : lat // 2], held.at[4, 0 : lat // 2], y_next)
            back = send(held.at[3, lat // 2 : lat], held.at[4, lat // 2 : lat], y_back)
        return ahead, back

    hand = hand_hop(1)

    rows[0:CAP, :] = picked_rows[0:CAP, :]
    for j in range(1, experts):
        dispatch[j - 1].wait_recv()
        rows[CAP * j : CAP * (j + 1), :] = landed[j]

    block = CAP * experts

    def place(ref, number, first=0, last=block, start=0, stop=None):
        stop = width if stop is None else stop
        return ref.at[number * block + first : number * block + last, start:stop]

    def part_of(hops, way):
        if hops < 4:
            return 0, block
        return (0, block // 2) if way == 0 else (block // 2, block)

    def own_hop(hops, way):
        first, last = part_of(hops, way)
        return send(
            place(rows, slot(0, way, hops - 1), first, last),
            place(rows, slot(0, way, hops), first, last),
            ways[way],
        )

    def other_hop(hops, way):
        first, last = part_of(hops, way)
        return send(
            place(rows, slot(1, way, hops - 1), first, last, 0, SPLIT),
            place(rows, slot(1, way, hops), first, last, 0, SPLIT),
            ways[way],
        )

    def cross_hop(hops, way):
        first, last = part_of(hops, way)
        start = 0 if hops == 0 else SPLIT
        return send(
            place(rows, slot(0, way, hops), first, last, start),
            place(rows, slot(1, way, hops), first, last, start),
            across,
        )

    for load in loads:
        load.wait()

    def feed_forward(first, last):
        size = last - first
        chunk = 512

        def inward(i, acc):
            cols = pl.ds(pl.multiple_of(i * chunk, chunk), chunk)
            return acc + jnp.dot(
                rows[first:last, cols], gate_up[cols, :], preferred_element_type=jnp.float32
            )

        acc = lax.fori_loop(0, width // chunk, inward, jnp.zeros((size, 256), jnp.float32))
        gate = acc[:, 0:128]
        hidden = (gate / (1.0 + jnp.exp(-gate)) * acc[:, 128:256]).astype(jnp.bfloat16)

        def outward(i, carry):
            cols = pl.ds(pl.multiple_of(i * chunk, chunk), chunk)
            parts[first:last, cols] = jnp.dot(
                hidden, down[:, cols], preferred_element_type=jnp.float32
            ).astype(jnp.bfloat16)
            return carry

        lax.fori_loop(0, width // chunk, outward, 0)

    for r in range(fresh.shape[0]):
        fresh[r] = jnp.zeros(fresh.shape[1:], fresh.dtype)
        fresh[r, 0 : new_ref.shape[1], :] = new_ref[r]
    reqs = cache.shape[0]
    kv = lat - ROPE
    steps = new_ref.shape[1]
    heads = query.shape[1] // steps
    device = (section * experts + expert) * (2 * RING) + dp
    source = source_ref[0, dp]
    source_across = source_ref[0, (1 - x) * RING + y]

    def attend(r, keys, length):
        queries = query[r]
        over_last = (((1,), (1,)), ((), ()))
        scores = softmax_scale * jnp.dot(queries, keys[...], preferred_element_type=jnp.float32)
        new_scores = softmax_scale * lax.dot_general(
            queries, fresh[r], over_last, preferred_element_type=jnp.float32
        )
        lane = lax.broadcasted_iota(jnp.int32, scores.shape, 1)
        new_lane = lax.broadcasted_iota(jnp.int32, new_scores.shape, 1)
        step = lax.broadcasted_iota(jnp.int32, new_scores.shape, 0) // heads
        scores = jnp.where(lane < length, scores, -jnp.inf)
        new_scores = jnp.where(new_lane <= step, new_scores, -jnp.inf)
        top = jnp.maximum(
            jnp.max(scores, axis=1, keepdims=True), jnp.max(new_scores, axis=1, keepdims=True)
        )
        weights = jnp.exp(scores - top)
        new_weights = jnp.exp(new_scores - top)
        total = jnp.sum(weights, axis=1, keepdims=True) + jnp.sum(
            new_weights, axis=1, keepdims=True
        )
        context = lax.dot_general(
            (weights / total).astype(jnp.bfloat16),
            keys[0:kv, :],
            over_last,
            preferred_element_type=jnp.float32,
        ) + jnp.dot(
            (new_weights / total).astype(jnp.bfloat16),
            fresh[r, :, 0:kv],
            preferred_element_type=jnp.float32,
        )
        context_ref[r] = context.astype(jnp.bfloat16)

    own = {}
    other = {}
    crossing = {}
    crossing[0, 0] = cross_hop(0, 0)
    for way in (0, 1):
        own[1, way] = own_hop(1, way)
    crossing[0, 0].wait_recv()
    for way in (0, 1):
        other[1, way] = other_hop(1, way)
    for arrived in hand:
        arrived.wait_recv()
    hand = hand_hop(2)

    bounds = {1: (0, 6 * block), 2: (6 * block, 10 * block)}
    for hops in (1, 2, 3, 4):
        for way in (0, 1):
            own[hops, way].wait_recv()
            if hops < 4:
                own[hops + 1, way] = own_hop(hops + 1, way)
            crossing[hops, way] = cross_hop(hops, way)
        for way in (0, 1):
            other[hops, way].wait_recv()
            if hops < 4:
                other[hops + 1, way] = other_hop(hops + 1, way)
        if hops > 1 and hops < 4:
            for way in (0, 1):
                crossing[hops - 1, way].wait_recv()
            feed_forward(*bounds[hops - 1])
            attend(hops - 2, cache.at[hops - 2], len_ref[device * reqs + hops - 2])
    for arrived in hand:
        arrived.wait_recv()
    hand = hand_hop(3)
    for hops in (3, 4):
        for way in (0, 1):
            crossing[hops, way].wait_recv()
    feed_forward(10 * block, 16 * block)

    over_x = {}

    def sum_cross(hops, way):
        first, last = part_of(hops, way)
        start = number_of(hops, way)
        return send(
            place(parts, slot(1, way, hops), first, last, SPLIT),
            from_x.at[start * block + first : start * block + last, :],
            across,
        )

    def number_of(hops, way):
        if hops == 0:
            return 0
        if hops == 4:
            return 7
        return 1 + (hops - 1) * 2 + way

    def take_cross(hops, way):
        over_x[hops, way].wait_recv()
        first, last = part_of(hops, way)
        start = number_of(hops, way)
        base = slot(0, way, hops) * block
        add_rows(
            parts,
            slice(base + first, base + last),
            from_x,
            slice(start * block + first, start * block + last),
            SPLIT,
            width,
        )

    def sum_hop(hops, way, col):
        first, last = part_of(hops, way)
        stop = width if col == 0 else SPLIT
        landing = from_y if col == 0 else from_y_other
        start = (hops - 1) * 2 + way
        return send(
            place(parts, slot(col, way, hops), first, last, 0, stop),
            landing.at[start * block + first : start * block + last, :],
            homeward[way],
        )

    def take_hop(copy, hops, way, col):
        copy.wait_recv()
        first, last = part_of(hops, way)
        stop = width if col == 0 else SPLIT
        landing = from_y if col == 0 else from_y_other
        start = (hops - 1) * 2 + way
        base = slot(col, way, hops - 1) * block
        add_rows(
            parts,
            slice(base + first, base + last),
            landing,
            slice(start * block + first, start * block + last),
            0,
            stop,
        )

    home = {}
    for hops in (4, 3, 2, 1):
        for way in (0, 1):
            over_x[hops, way] = sum_cross(hops, way)
    over_x[0, 0] = sum_cross(0, 0)
    for way in (0, 1):
        home[4, way, 1] = sum_hop(4, way, 1)
    for way in (0, 1):
        take_cross(4, way)
        home[4, way, 0] = sum_hop(4, way, 0)
    for hops in (3, 2, 1):
        for way in (0, 1):
            take_hop(home[hops + 1, way, 1], hops + 1, way, 1)
            home[hops, way, 1] = sum_hop(hops, way, 1)
        for way in (0, 1):
            take_cross(hops, way)
        for way in (0, 1):
            take_hop(home[hops + 1, way, 0], hops + 1, way, 0)
            home[hops, way, 0] = sum_hop(hops, way, 0)
        if hops == 3:
            for arrived in hand:
                arrived.wait_recv()
            hand = hand_hop(4)
        if hops == 2:
            for arrived in hand:
                arrived.wait_recv()
            pick_out[...] = held[lax.rem(lax.rem(source_across, RING) - y + RING, RING)]
            pick_pair[0] = held[lax.rem(lax.rem(source, RING) - y + RING, RING)]
            swap = send(pick_out, pick_pair.at[1], across)
    take_cross(0, 0)
    for way in (0, 1):
        take_hop(home[1, way, 1], 1, way, 1)
    last_cross = send(place(parts, slot(1, 0, 0), 0, block, 0, SPLIT), from_x_last, across)
    for way in (0, 1):
        take_hop(home[1, way, 0], 1, way, 0)
    last_cross.wait_recv()
    add_rows(parts, slice(0, block), from_x_last, slice(0, block), 0, SPLIT)

    back = []
    for j in range(1, experts):
        going[j] = parts[CAP * j : CAP * (j + 1), :]
        back.append(
            send(going.at[j], coming.at[j], {"expert": lax.rem(expert + experts - j, experts)})
        )
    picked_rows[0:CAP, :] = parts[0:CAP, :]

    swap.wait_recv()
    picked[...] = pick_pair[jnp.where(source // RING == x, 0, 1)]
    second_cross = copy_to(picked, handed_half, other_section)
    handed[:, half : 2 * half] = picked[...]

    @pl.when(section == 0)
    def _():
        second_cross.start()
        handed[:, 0:half] = picked[...]

    @pl.when(section == 1)
    def _():
        second_cross.wait_recv()
        handed[:, 0:half] = handed_half[...]

    source_row = (expert * 2 * RING + source) * reqs + hand_slot_ref[0, dp]
    attend(reqs, handed, jnp.where(section == 1, len_ref[source_row], 0))

    for j in range(1, experts):
        back[j - 1].wait_recv()
        picked_rows[CAP * j : CAP * (j + 1), :] = coming[j]
    moe_ref[...] = lax.dot_general(
        mixing,
        picked_rows[...].astype(jnp.float32),
        (((0,), (0,)), ((), ())),
        precision=highest,
    ).astype(jnp.bfloat16)

    for copy in sent:
        copy.wait_send()

    @pl.when(section == 0)
    def _():
        first_cross.wait_send()
        second_cross.wait_send()


def shards(
    tokens,
    route_ids,
    route_weight,
    gate_weight,
    up_weight,
    down_weight,
    latent_cache,
    cache_len,
    hand_source,
    hand_slot,
    query_latent,
    new_latent,
):
    tok_rows, width = tokens.shape
    experts = lax.axis_size("expert")
    slot_count, step_count, _ = query_latent.shape
    requests, max_len, lat = latent_cache.shape
    lane_rows = experts * CAP
    half = max_len // 2
    kv = lat - ROPE
    query_rows = query_latent.shape[1] * query_latent.shape[2] // lat
    queries = query_latent.reshape(slot_count, query_rows, lat)
    bf16 = jnp.bfloat16
    smem = pl.BlockSpec(memory_space=pltpu.SMEM)
    vmem = pl.BlockSpec(memory_space=pltpu.VMEM)
    anywhere = pl.BlockSpec(memory_space=pl.ANY)
    moe_out, context = pl.pallas_call(
        exchange,
        out_shape=(
            jax.ShapeDtypeStruct((tok_rows, width), bf16),
            jax.ShapeDtypeStruct((slot_count, query_rows, kv), bf16),
        ),
        in_specs=[smem] * 3 + [vmem] * 4 + [anywhere] * 5,
        out_specs=(vmem, vmem),
        scratch_shapes=[
            pltpu.VMEM((lane_rows, width), bf16),
            pltpu.VMEM((experts, CAP, width), bf16),
            pltpu.VMEM((experts, CAP, width), bf16),
            pltpu.VMEM((16 * lane_rows, width), bf16),
            pltpu.VMEM((16 * lane_rows, width), bf16),
            pltpu.VMEM((8 * lane_rows, width), bf16),
            pltpu.VMEM((8 * lane_rows, SPLIT), bf16),
            pltpu.VMEM((8 * lane_rows, width - SPLIT), bf16),
            pltpu.VMEM((lane_rows, SPLIT), bf16),
            pltpu.VMEM((experts, CAP, width), bf16),
            pltpu.VMEM((experts, CAP, width), bf16),
            pltpu.VMEM((requests, lat, max_len), bf16),
            pltpu.VMEM((slot_count, query_rows, lat), bf16),
            pltpu.VMEM((slot_count, 16, lat), bf16),
            pltpu.VMEM((lat, max_len), bf16),
            pltpu.VMEM((RING, lat, half), bf16),
            pltpu.VMEM((2, lat, half), bf16),
            pltpu.VMEM((lat, half), bf16),
            pltpu.VMEM((lat, half), bf16),
            pltpu.VMEM((lat, half), bf16),
            pltpu.VMEM((lat, max_len), bf16),
            pltpu.VMEM((width, 256), bf16),
            pltpu.VMEM((128, width), bf16),
            pltpu.SemaphoreType.DMA((100,)),
            pltpu.SemaphoreType.DMA((100,)),
            pltpu.SemaphoreType.DMA((5,)),
        ],
        compiler_params=pltpu.CompilerParams(
            collective_id=0, has_side_effects=True, vmem_limit_bytes=48 * 1024 * 1024
        ),
    )(
        hand_source,
        hand_slot,
        cache_len,
        tokens,
        route_ids.T,
        route_weight.T,
        new_latent,
        jnp.swapaxes(latent_cache, 1, 2),
        queries,
        gate_weight[0],
        up_weight[0],
        down_weight[0],
    )
    return (moe_out, context.reshape(slot_count, step_count, query_rows // step_count * kv))


def solution(mesh):
    return jax.shard_map(
        shards,
        mesh=mesh,
        in_specs=(
            P(("section", "expert", "dp"), None),
            P(("section", "expert", "dp"), None),
            P(("section", "expert", "dp"), None),
            P(("section", "expert"), None, "dp"),
            P(("section", "expert"), None, "dp"),
            P(("section", "expert"), "dp", None),
            P(("section", "expert", "dp"), None, None),
            P(),
            P("expert", None),
            P("expert", None),
            P(("section", "expert", "dp"), None, None),
            P(("section", "expert", "dp"), None, None),
        ),
        out_specs=(
            P(("section", "expert", "dp"), None),
            P(("section", "expert", "dp"), None, None),
        ),
        check_vma=False,
    )
```

```python
import jax
import jax.numpy as jnp
from jax import lax
from jax.experimental import pallas as pl
from jax.experimental.pallas import tpu as pltpu
from jax.sharding import PartitionSpec as P

CAP = 2
ROPE = 64
RING = 8
SPLIT = 1536
MESH = pl.DeviceIdType.MESH

softmax_scale = 192.0 ** (-0.5)
highest = lax.Precision.HIGHEST


def slot(col, way, hops):
    if hops == 0:
        return col
    if hops == 4:
        return 14 + col
    return 2 + (hops - 1) * 4 + col * 2 + way


def exchange(
    source_ref,
    hand_slot_ref,
    len_ref,
    tokens_ref,
    ids_ref,
    weight_ref,
    new_ref,
    cache_ref,
    query_ref,
    gate_ref,
    up_ref,
    down_ref,
    moe_ref,
    context_ref,
    picked_rows,
    leaving,
    landed,
    rows,
    parts,
    from_y,
    from_y_other,
    from_x,
    from_x_last,
    going,
    coming,
    cache,
    query,
    fresh,
    chosen,
    held,
    pick_pair,
    pick_out,
    picked,
    handed_half,
    handed,
    gate_up,
    down,
    send_sem,
    recv_sem,
    local_sem,
):
    width = rows.shape[2]
    section = lax.axis_index("section")
    expert = lax.axis_index("expert")
    dp = lax.axis_index("dp")
    experts = leaving.shape[0]
    x = dp // RING
    y = lax.rem(dp, RING)
    y_next = {"dp": x * RING + lax.rem(y + 1, RING)}
    y_back = {"dp": x * RING + lax.rem(y + RING - 1, RING)}
    across = {"dp": (1 - x) * RING + y}
    other_section = {"section": 1 - section}
    ways = (y_next, y_back)
    homeward = (y_back, y_next)

    loads = [
        pltpu.make_async_copy(gate_ref, gate_up.at[:, 0:128], local_sem.at[0]),
        pltpu.make_async_copy(up_ref, gate_up.at[:, 128:256], local_sem.at[1]),
        pltpu.make_async_copy(down_ref, down, local_sem.at[2]),
        pltpu.make_async_copy(query_ref, query, local_sem.at[3]),
    ]
    cache_load = pltpu.make_async_copy(cache_ref, cache, local_sem.at[4])
    cache_load.start()
    for load in loads:
        load.start()

    barrier = pltpu.get_barrier_semaphore()
    for peer in (y_next, y_back, across, other_section):
        pl.semaphore_signal(barrier, inc=1, device_id=peer, device_id_type=MESH)
    for j in range(1, experts):
        peer = {"expert": lax.rem(expert + j, experts)}
        pl.semaphore_signal(barrier, inc=1, device_id=peer, device_id_type=MESH)

    choices, tok_rows = ids_ref.shape
    slots = experts * CAP
    relative = lax.rem(ids_ref[...] - expert + experts, experts)
    slot_row = lax.broadcasted_iota(jnp.int32, (slots, tok_rows), 0)
    hits = jnp.zeros((slots, tok_rows), jnp.float32)
    mixing = jnp.zeros((slots, tok_rows), jnp.float32)
    for k in range(choices):
        hit = relative[k : k + 1, :] == slot_row // CAP
        hits = hits + jnp.where(hit, 1.0, 0.0)
        mixing = mixing + jnp.where(hit, weight_ref[k : k + 1, :], 0.0)
    token_row = lax.broadcasted_iota(jnp.int32, (tok_rows, tok_rows), 0)
    token_lane = lax.broadcasted_iota(jnp.int32, (tok_rows, tok_rows), 1)
    before = jnp.where(token_row < token_lane, 1.0, 0.0)
    earlier = jnp.dot(
        hits.astype(jnp.bfloat16), before.astype(jnp.bfloat16), preferred_element_type=jnp.float32
    )
    taken = jnp.where(earlier == lax.rem(slot_row, CAP).astype(jnp.float32), hits, 0.0)
    mixing = mixing * taken
    picked_rows[...] = jnp.dot(
        taken.astype(jnp.bfloat16), tokens_ref[...], preferred_element_type=jnp.float32
    ).astype(jnp.bfloat16)
    for j in range(1, experts):
        leaving[j] = picked_rows[CAP * j : CAP * (j + 1), :]
    pl.semaphore_wait(barrier, 4 + experts - 1)

    count = [0]
    sent = []

    def copy_to(src, dst, device):
        number = count[0]
        count[0] += 1
        return pltpu.make_async_remote_copy(
            src_ref=src,
            dst_ref=dst,
            send_sem=send_sem.at[number],
            recv_sem=recv_sem.at[number],
            device_id=device,
            device_id_type=MESH,
        )

    def send(src, dst, device):
        copy = copy_to(src, dst, device)
        copy.start()
        sent.append(copy)
        return copy

    dispatch = {}
    for j in (1, 15, 2, 14, 3, 13, 4, 12, 5, 11, 6, 10, 7, 9, 8):
        peer = {"expert": lax.rem(expert + j, experts)}
        dispatch[j] = send(leaving.at[j], landed.at[j], peer)

    chosen_slot = 0
    for j in range(2 * RING):
        chosen_slot += jnp.where(source_ref[0, j] == dp, hand_slot_ref[0, j], 0)
    cache_load.wait()
    chosen[...] = cache[chosen_slot]
    half = held.shape[2]
    lat = held.shape[1]
    first_cross = copy_to(chosen.at[:, half : 2 * half], held.at[0], other_section)

    @pl.when(section == 0)
    def _():
        first_cross.start()
        held[0] = chosen[:, 0:half]

    @pl.when(section == 1)
    def _():
        first_cross.wait_recv()

    def hand_hop(hops):
        if hops < 4:
            ahead = send(held.at[(RING - hops + 1) % RING], held.at[RING - hops], y_next)
            back = send(held.at[hops - 1], held.at[hops], y_back)
        else:
            ahead = send(held.at[RING - 3, 0 : lat // 2], held.at[4, 0 : lat // 2], y_next)
            back = send(held.at[3, lat // 2 : lat], held.at[4, lat // 2 : lat], y_back)
        return ahead, back

    hand = hand_hop(1)

    order = ((0, 1, 15, 2, 14, 3, 13, 4), (12, 5, 11, 6, 10, 7, 9, 8))
    block = rows.shape[1] // (2 * RING)

    def land(h):
        for i, j in enumerate(order[h]):
            if j == 0:
                rows[h, CAP * i : CAP * (i + 1), :] = picked_rows[0:CAP, :]
            else:
                dispatch[j].wait_recv()
                rows[h, CAP * i : CAP * (i + 1), :] = landed[j]

    def place(ref, h, number, start=0, stop=None):
        stop = width if stop is None else stop
        return ref.at[h, number * block : (number + 1) * block, start:stop]

    def ways_at(hops, h):
        return (0, 1) if hops < 4 else (h,)

    own = {}
    other = {}
    crossing = {}

    def own_hop(h, hops, way):
        own[h, hops, way] = send(
            place(rows, h, slot(0, way, hops - 1)), place(rows, h, slot(0, way, hops)), ways[way]
        )

    def other_hop(h, hops, way):
        other[h, hops, way] = send(
            place(rows, h, slot(1, way, hops - 1), 0, SPLIT),
            place(rows, h, slot(1, way, hops), 0, SPLIT),
            ways[way],
        )

    def cross_hop(h, hops, way):
        start = 0 if hops == 0 else SPLIT
        crossing[h, hops, way] = send(
            place(rows, h, slot(0, way, hops), start),
            place(rows, h, slot(1, way, hops), start),
            across,
        )

    def gather_start(h):
        cross_hop(h, 0, 0)
        for way in (0, 1):
            own_hop(h, 1, way)

    def gather_other(h):
        crossing[h, 0, 0].wait_recv()
        for way in (0, 1):
            other_hop(h, 1, way)

    def gather_step(h, hops):
        for way in ways_at(hops, h):
            own[h, hops, way].wait_recv()
            if hops < 4 and way in ways_at(hops + 1, h):
                own_hop(h, hops + 1, way)
            cross_hop(h, hops, way)
        for way in ways_at(hops, h):
            other[h, hops, way].wait_recv()
            if hops < 4 and way in ways_at(hops + 1, h):
                other_hop(h, hops + 1, way)

    def feed_forward(h, first, last):
        size = last - first
        chunk = 512

        def inward(i, acc):
            cols = pl.ds(pl.multiple_of(i * chunk, chunk), chunk)
            return acc + jnp.dot(
                rows[h, first:last, cols], gate_up[cols, :], preferred_element_type=jnp.float32
            )

        acc = lax.fori_loop(0, width // chunk, inward, jnp.zeros((size, 256), jnp.float32))
        gate = acc[:, 0:128]
        hidden = (gate / (1.0 + jnp.exp(-gate)) * acc[:, 128:256]).astype(jnp.bfloat16)

        def outward(i, carry):
            cols = pl.ds(pl.multiple_of(i * chunk, chunk), chunk)
            parts[h, first:last, cols] = jnp.dot(
                hidden, down[:, cols], preferred_element_type=jnp.float32
            ).astype(jnp.bfloat16)
            return carry

        lax.fori_loop(0, width // chunk, outward, 0)

    def near_experts(h):
        for hops in (1, 2):
            for way in (0, 1):
                crossing[h, hops, way].wait_recv()
        feed_forward(h, 0, 10 * block)

    def far_experts(h):
        for hops in (3, 4):
            for way in ways_at(hops, h):
                crossing[h, hops, way].wait_recv()
        feed_forward(h, 10 * block, 16 * block)

    over_x = {}
    home = {}
    last_cross = {}

    def number_of(hops, way):
        if hops == 0:
            return 0
        if hops == 4:
            return 7
        return 1 + (hops - 1) * 2 + way

    def sum_cross(h, hops, way):
        over_x[h, hops, way] = send(
            place(parts, h, slot(1, way, hops), SPLIT),
            place(from_x, h, number_of(hops, way), 0, width - SPLIT),
            across,
        )

    def take_cross(h, hops, way):
        over_x[h, hops, way].wait_recv()
        add_block(parts, h, slot(0, way, hops), from_x, number_of(hops, way), SPLIT, width)

    def sum_hop(h, hops, way, col):
        stop = width if col == 0 else SPLIT
        landing = from_y if col == 0 else from_y_other
        home[h, hops, way, col] = send(
            place(parts, h, slot(col, way, hops), 0, stop),
            place(landing, h, (hops - 1) * 2 + way, 0, stop),
            homeward[way],
        )

    def take_hop(h, hops, way, col):
        home[h, hops, way, col].wait_recv()
        stop = width if col == 0 else SPLIT
        landing = from_y if col == 0 else from_y_other
        add_block(parts, h, slot(col, way, hops - 1), landing, (hops - 1) * 2 + way, 0, stop)

    def add_block(target, h, number, source_of, source_number, start, stop):
        chunk = 512
        to_rows = pl.ds(number * block, block)
        from_rows = pl.ds(source_number * block, block)

        def body(i, carry):
            cols = pl.ds(pl.multiple_of(start + i * chunk, chunk), chunk)
            from_cols = pl.ds(pl.multiple_of(i * chunk, chunk), chunk)
            total = target[h, to_rows, cols].astype(jnp.float32) + source_of[
                h, from_rows, from_cols
            ].astype(jnp.float32)
            target[h, to_rows, cols] = total.astype(jnp.bfloat16)
            return carry

        lax.fori_loop(0, (stop - start) // chunk, body, 0)

    def sum_start(h):
        for hops in (4, 3, 2, 1):
            for way in ways_at(hops, h)[:: 1 if h else -1]:
                sum_cross(h, hops, way)
        sum_cross(h, 0, 0)
        sum_hop(h, 4, h, 1)
        sum_hop(h, 3, 1 - h, 1)
        take_cross(h, 4, h)
        sum_hop(h, 4, h, 0)
        take_cross(h, 3, 1 - h)
        sum_hop(h, 3, 1 - h, 0)

    def sum_step(h, hops):
        going_on = (0, 1) if hops < 3 else (h,)
        for way in going_on:
            take_hop(h, hops + 1, way, 1)
            sum_hop(h, hops, way, 1)
        for way in going_on:
            take_cross(h, hops, way)
        for way in going_on:
            take_hop(h, hops + 1, way, 0)
            sum_hop(h, hops, way, 0)

    def sum_end(h):
        take_cross(h, 0, 0)
        for way in (0, 1):
            take_hop(h, 1, way, 1)
        last_cross[h] = send(place(parts, h, 1, 0, SPLIT), place(from_x_last, h, 0, 0, SPLIT), across)
        for way in (0, 1):
            take_hop(h, 1, way, 0)

    for r in range(fresh.shape[0]):
        fresh[r] = jnp.zeros(fresh.shape[1:], fresh.dtype)
        fresh[r, 0 : new_ref.shape[1], :] = new_ref[r]
    reqs = cache.shape[0]
    kv = lat - ROPE
    steps = new_ref.shape[1]
    heads = query.shape[1] // steps
    device = (section * experts + expert) * (2 * RING) + dp
    source = source_ref[0, dp]
    source_across = source_ref[0, (1 - x) * RING + y]

    def attend(r, keys, length):
        queries = query[r]
        over_last = (((1,), (1,)), ((), ()))
        scores = softmax_scale * jnp.dot(queries, keys[...], preferred_element_type=jnp.float32)
        new_scores = softmax_scale * lax.dot_general(
            queries, fresh[r], over_last, preferred_element_type=jnp.float32
        )
        lane = lax.broadcasted_iota(jnp.int32, scores.shape, 1)
        new_lane = lax.broadcasted_iota(jnp.int32, new_scores.shape, 1)
        step = lax.broadcasted_iota(jnp.int32, new_scores.shape, 0) // heads
        scores = jnp.where(lane < length, scores, -jnp.inf)
        new_scores = jnp.where(new_lane <= step, new_scores, -jnp.inf)
        top = jnp.maximum(
            jnp.max(scores, axis=1, keepdims=True), jnp.max(new_scores, axis=1, keepdims=True)
        )
        weights = jnp.exp(scores - top)
        new_weights = jnp.exp(new_scores - top)
        total = jnp.sum(weights, axis=1, keepdims=True) + jnp.sum(
            new_weights, axis=1, keepdims=True
        )
        context = lax.dot_general(
            (weights / total).astype(jnp.bfloat16),
            keys[0:kv, :],
            over_last,
            preferred_element_type=jnp.float32,
        ) + jnp.dot(
            (new_weights / total).astype(jnp.bfloat16),
            fresh[r, :, 0:kv],
            preferred_element_type=jnp.float32,
        )
        context_ref[r] = context.astype(jnp.bfloat16)

    land(0)
    gather_start(0)
    land(1)
    gather_start(1)
    for load in loads:
        load.wait()
    gather_other(0)
    gather_other(1)
    for arrived in hand:
        arrived.wait_recv()
    hand = hand_hop(2)
    for hops in (1, 2):
        for h in (0, 1):
            gather_step(h, hops)
        attend(hops - 1, cache.at[hops - 1], len_ref[device * reqs + hops - 1])
    for h in (0, 1):
        gather_step(h, 3)
        near_experts(h)
    for h in (0, 1):
        gather_step(h, 4)
    for arrived in hand:
        arrived.wait_recv()
    hand = hand_hop(3)
    for h in (0, 1):
        far_experts(h)
        sum_start(h)
    for h in (0, 1):
        sum_step(h, 3)
    for arrived in hand:
        arrived.wait_recv()
    hand = hand_hop(4)
    for h in (0, 1):
        sum_step(h, 2)
    for arrived in hand:
        arrived.wait_recv()
    pick_out[...] = held[lax.rem(lax.rem(source_across, RING) - y + RING, RING)]
    pick_pair[0] = held[lax.rem(lax.rem(source, RING) - y + RING, RING)]
    swap = send(pick_out, pick_pair.at[1], across)
    for h in (0, 1):
        sum_step(h, 1)
    for h in (0, 1):
        sum_end(h)

    back = {}
    for h in (0, 1):
        last_cross[h].wait_recv()
        add_block(parts, h, 0, from_x_last, 0, 0, SPLIT)
        for i, j in enumerate(order[h]):
            if j == 0:
                picked_rows[0:CAP, :] = parts[h, CAP * i : CAP * (i + 1), :]
            else:
                going[j] = parts[h, CAP * i : CAP * (i + 1), :]
                back[j] = send(
                    going.at[j], coming.at[j], {"expert": lax.rem(expert + experts - j, experts)}
                )

    swap.wait_recv()
    picked[...] = pick_pair[jnp.where(source // RING == x, 0, 1)]
    second_cross = copy_to(picked, handed_half, other_section)
    handed[:, half : 2 * half] = picked[...]

    @pl.when(section == 0)
    def _():
        second_cross.start()
        handed[:, 0:half] = picked[...]

    @pl.when(section == 1)
    def _():
        second_cross.wait_recv()
        handed[:, 0:half] = handed_half[...]

    source_row = (expert * 2 * RING + source) * reqs + hand_slot_ref[0, dp]
    attend(reqs, handed, jnp.where(section == 1, len_ref[source_row], 0))

    for j in range(1, experts):
        back[j].wait_recv()
        picked_rows[CAP * j : CAP * (j + 1), :] = coming[j]
    moe_ref[...] = lax.dot_general(
        mixing,
        picked_rows[...].astype(jnp.float32),
        (((0,), (0,)), ((), ())),
        precision=highest,
    ).astype(jnp.bfloat16)

    for copy in sent:
        copy.wait_send()

    @pl.when(section == 0)
    def _():
        first_cross.wait_send()
        second_cross.wait_send()


def shards(
    tokens,
    route_ids,
    route_weight,
    gate_weight,
    up_weight,
    down_weight,
    latent_cache,
    cache_len,
    hand_source,
    hand_slot,
    query_latent,
    new_latent,
):
    tok_rows, width = tokens.shape
    experts = lax.axis_size("expert")
    slot_count, step_count, _ = query_latent.shape
    requests, max_len, lat = latent_cache.shape
    lane_rows = experts * CAP
    half = max_len // 2
    kv = lat - ROPE
    query_rows = query_latent.shape[1] * query_latent.shape[2] // lat
    queries = query_latent.reshape(slot_count, query_rows, lat)
    bf16 = jnp.bfloat16
    smem = pl.BlockSpec(memory_space=pltpu.SMEM)
    vmem = pl.BlockSpec(memory_space=pltpu.VMEM)
    anywhere = pl.BlockSpec(memory_space=pl.ANY)
    moe_out, context = pl.pallas_call(
        exchange,
        out_shape=(
            jax.ShapeDtypeStruct((tok_rows, width), bf16),
            jax.ShapeDtypeStruct((slot_count, query_rows, kv), bf16),
        ),
        in_specs=[smem] * 3 + [vmem] * 4 + [anywhere] * 5,
        out_specs=(vmem, vmem),
        scratch_shapes=[
            pltpu.VMEM((lane_rows, width), bf16),
            pltpu.VMEM((experts, CAP, width), bf16),
            pltpu.VMEM((experts, CAP, width), bf16),
            pltpu.VMEM((2, 8 * lane_rows, width), bf16),
            pltpu.VMEM((2, 8 * lane_rows, width), bf16),
            pltpu.VMEM((2, 4 * lane_rows, width), bf16),
            pltpu.VMEM((2, 4 * lane_rows, SPLIT), bf16),
            pltpu.VMEM((2, 4 * lane_rows, width - SPLIT), bf16),
            pltpu.VMEM((2, lane_rows // 2, SPLIT), bf16),
            pltpu.VMEM((experts, CAP, width), bf16),
            pltpu.VMEM((experts, CAP, width), bf16),
            pltpu.VMEM((requests, lat, max_len), bf16),
            pltpu.VMEM((slot_count, query_rows, lat), bf16),
            pltpu.VMEM((slot_count, 16, lat), bf16),
            pltpu.VMEM((lat, max_len), bf16),
            pltpu.VMEM((RING, lat, half), bf16),
            pltpu.VMEM((2, lat, half), bf16),
            pltpu.VMEM((lat, half), bf16),
            pltpu.VMEM((lat, half), bf16),
            pltpu.VMEM((lat, half), bf16),
            pltpu.VMEM((lat, max_len), bf16),
            pltpu.VMEM((width, 256), bf16),
            pltpu.VMEM((128, width), bf16),
            pltpu.SemaphoreType.DMA((160,)),
            pltpu.SemaphoreType.DMA((160,)),
            pltpu.SemaphoreType.DMA((5,)),
        ],
        compiler_params=pltpu.CompilerParams(
            collective_id=0, has_side_effects=True, vmem_limit_bytes=62 * 1024 * 1024
        ),
    )(
        hand_source,
        hand_slot,
        cache_len,
        tokens,
        route_ids.T,
        route_weight.T,
        new_latent,
        jnp.swapaxes(latent_cache, 1, 2),
        queries,
        gate_weight[0],
        up_weight[0],
        down_weight[0],
    )
    return (moe_out, context.reshape(slot_count, step_count, query_rows // step_count * kv))


def solution(mesh):
    return jax.shard_map(
        shards,
        mesh=mesh,
        in_specs=(
            P(("section", "expert", "dp"), None),
            P(("section", "expert", "dp"), None),
            P(("section", "expert", "dp"), None),
            P(("section", "expert"), None, "dp"),
            P(("section", "expert"), None, "dp"),
            P(("section", "expert"), "dp", None),
            P(("section", "expert", "dp"), None, None),
            P(),
            P("expert", None),
            P("expert", None),
            P(("section", "expert", "dp"), None, None),
            P(("section", "expert", "dp"), None, None),
        ),
        out_specs=(
            P(("section", "expert", "dp"), None),
            P(("section", "expert", "dp"), None, None),
        ),
        check_vma=False,
    )
```

```python
import jax
import jax.numpy as jnp
from jax import lax
from jax.experimental import pallas as pl
from jax.experimental.pallas import tpu as pltpu
from jax.sharding import PartitionSpec as P

CAP = 2
ROPE = 64
RING = 8
SPLIT = 1536
MESH = pl.DeviceIdType.MESH

softmax_scale = 192.0 ** (-0.5)
highest = lax.Precision.HIGHEST


def slot(col, way, hops):
    if hops == 0:
        return col
    if hops == 4:
        return 14 + col
    return 2 + (hops - 1) * 4 + col * 2 + way


def exchange(
    source_ref,
    hand_slot_ref,
    len_ref,
    tokens_ref,
    ids_ref,
    weight_ref,
    new_ref,
    cache_ref,
    query_ref,
    gate_ref,
    up_ref,
    down_ref,
    moe_ref,
    context_ref,
    picked_rows,
    leaving,
    landed,
    rows,
    parts,
    from_y,
    from_y_other,
    from_x,
    from_x_last,
    going,
    coming,
    cache,
    query,
    fresh_even,
    fresh_odd,
    even,
    odd,
    context,
    chosen,
    held,
    pick_pair,
    pick_out,
    picked,
    handed_half,
    handed,
    gate_up,
    down,
    send_sem,
    recv_sem,
    local_sem,
):
    width = rows.shape[2]
    section = lax.axis_index("section")
    expert = lax.axis_index("expert")
    dp = lax.axis_index("dp")
    experts = leaving.shape[0]
    x = dp // RING
    y = lax.rem(dp, RING)
    y_next = {"dp": x * RING + lax.rem(y + 1, RING)}
    y_back = {"dp": x * RING + lax.rem(y + RING - 1, RING)}
    across = {"dp": (1 - x) * RING + y}
    other_section = {"section": 1 - section}
    ways = (y_next, y_back)
    homeward = (y_back, y_next)

    loads = [
        pltpu.make_async_copy(gate_ref, gate_up.at[:, 0:128], local_sem.at[0]),
        pltpu.make_async_copy(up_ref, gate_up.at[:, 128:256], local_sem.at[1]),
        pltpu.make_async_copy(down_ref, down, local_sem.at[2]),
        pltpu.make_async_copy(query_ref, query, local_sem.at[3]),
    ]
    cache_load = pltpu.make_async_copy(
        cache_ref, cache.at[:, ROPE : ROPE + cache_ref.shape[1]], local_sem.at[4]
    )
    cache_load.start()
    for load in loads:
        load.start()

    barrier = pltpu.get_barrier_semaphore()
    for peer in (y_next, y_back, across, other_section):
        pl.semaphore_signal(barrier, inc=1, device_id=peer, device_id_type=MESH)
    for j in range(1, experts):
        peer = {"expert": lax.rem(expert + j, experts)}
        pl.semaphore_signal(barrier, inc=1, device_id=peer, device_id_type=MESH)

    choices, tok_rows = ids_ref.shape
    slots = experts * CAP
    relative = lax.rem(ids_ref[...] - expert + experts, experts)
    slot_row = lax.broadcasted_iota(jnp.int32, (slots, tok_rows), 0)
    hits = jnp.zeros((slots, tok_rows), jnp.float32)
    mixing = jnp.zeros((slots, tok_rows), jnp.float32)
    for k in range(choices):
        hit = relative[k : k + 1, :] == slot_row // CAP
        hits = hits + jnp.where(hit, 1.0, 0.0)
        mixing = mixing + jnp.where(hit, weight_ref[k : k + 1, :], 0.0)
    token_row = lax.broadcasted_iota(jnp.int32, (tok_rows, tok_rows), 0)
    token_lane = lax.broadcasted_iota(jnp.int32, (tok_rows, tok_rows), 1)
    before = jnp.where(token_row < token_lane, 1.0, 0.0)
    earlier = jnp.dot(
        hits.astype(jnp.bfloat16), before.astype(jnp.bfloat16), preferred_element_type=jnp.float32
    )
    taken = jnp.where(earlier == lax.rem(slot_row, CAP).astype(jnp.float32), hits, 0.0)
    mixing = mixing * taken
    picked_rows[...] = jnp.dot(
        taken.astype(jnp.bfloat16), tokens_ref[...], preferred_element_type=jnp.float32
    ).astype(jnp.bfloat16)
    for j in range(1, experts):
        leaving[j] = picked_rows[CAP * j : CAP * (j + 1), :]
    pl.semaphore_wait(barrier, 4 + experts - 1)

    count = [0]
    sent = []

    def copy_to(src, dst, device):
        number = count[0]
        count[0] += 1
        return pltpu.make_async_remote_copy(
            src_ref=src,
            dst_ref=dst,
            send_sem=send_sem.at[number],
            recv_sem=recv_sem.at[number],
            device_id=device,
            device_id_type=MESH,
        )

    def send(src, dst, device):
        copy = copy_to(src, dst, device)
        copy.start()
        sent.append(copy)
        return copy

    dispatch = {}
    for j in (1, 15, 2, 14, 3, 13, 4, 12, 5, 11, 6, 10, 7, 9, 8):
        peer = {"expert": lax.rem(expert + j, experts)}
        dispatch[j] = send(leaving.at[j], landed.at[j], peer)

    chosen_slot = 0
    for j in range(2 * RING):
        chosen_slot += jnp.where(source_ref[0, j] == dp, hand_slot_ref[0, j], 0)
    cache_load.wait()
    chosen[...] = cache[chosen_slot, ROPE : ROPE + chosen.shape[0], :]
    half = held.shape[2]
    lat = held.shape[1]
    first_cross = copy_to(chosen.at[:, half : 2 * half], held.at[0], other_section)

    @pl.when(section == 0)
    def _():
        first_cross.start()
        held[0] = chosen[:, 0:half]

    @pl.when(section == 1)
    def _():
        first_cross.wait_recv()

    def hand_hop(hops):
        if hops < 4:
            ahead = send(held.at[(RING - hops + 1) % RING], held.at[RING - hops], y_next)
            back = send(held.at[hops - 1], held.at[hops], y_back)
        else:
            ahead = send(held.at[RING - 3, 0 : lat // 2], held.at[4, 0 : lat // 2], y_next)
            back = send(held.at[3, lat // 2 : lat], held.at[4, lat // 2 : lat], y_back)
        return ahead, back

    hand = hand_hop(1)

    order = ((0, 1, 15, 2, 14, 3, 13, 4), (12, 5, 11, 6, 10, 7, 9, 8))
    block = rows.shape[1] // (2 * RING)

    def land(h):
        for i, j in enumerate(order[h]):
            if j == 0:
                rows[h, CAP * i : CAP * (i + 1), :] = picked_rows[0:CAP, :]
            else:
                dispatch[j].wait_recv()
                rows[h, CAP * i : CAP * (i + 1), :] = landed[j]

    def place(ref, h, number, start=0, stop=None):
        stop = width if stop is None else stop
        return ref.at[h, number * block : (number + 1) * block, start:stop]

    def ways_at(hops, h):
        return (0, 1) if hops < 4 else (h,)

    own = {}
    other = {}
    crossing = {}

    def own_hop(h, hops, way):
        own[h, hops, way] = send(
            place(rows, h, slot(0, way, hops - 1)), place(rows, h, slot(0, way, hops)), ways[way]
        )

    def other_hop(h, hops, way):
        other[h, hops, way] = send(
            place(rows, h, slot(1, way, hops - 1), 0, SPLIT),
            place(rows, h, slot(1, way, hops), 0, SPLIT),
            ways[way],
        )

    def cross_hop(h, hops, way):
        start = 0 if hops == 0 else SPLIT
        crossing[h, hops, way] = send(
            place(rows, h, slot(0, way, hops), start),
            place(rows, h, slot(1, way, hops), start),
            across,
        )

    def gather_start(h):
        cross_hop(h, 0, 0)
        for way in (0, 1):
            own_hop(h, 1, way)

    def gather_other(h):
        crossing[h, 0, 0].wait_recv()
        for way in (0, 1):
            other_hop(h, 1, way)

    def gather_step(h, hops):
        for way in ways_at(hops, h):
            own[h, hops, way].wait_recv()
            if hops < 4 and way in ways_at(hops + 1, h):
                own_hop(h, hops + 1, way)
            cross_hop(h, hops, way)
        for way in ways_at(hops, h):
            other[h, hops, way].wait_recv()
            if hops < 4 and way in ways_at(hops + 1, h):
                other_hop(h, hops + 1, way)

    def feed_forward(h, first, last):
        chunk = 512
        acc = jnp.dot(rows[h, first:last, :], gate_up[...], preferred_element_type=jnp.float32)
        gate = acc[:, 0:128]
        hidden = (gate / (1.0 + jnp.exp(-gate)) * acc[:, 128:256]).astype(jnp.bfloat16)
        for start in range(0, width, chunk):
            parts[h, first:last, start : start + chunk] = jnp.dot(
                hidden, down[:, start : start + chunk], preferred_element_type=jnp.float32
            ).astype(jnp.bfloat16)

    def near_experts(h):
        for hops in (1, 2):
            for way in (0, 1):
                crossing[h, hops, way].wait_recv()
        feed_forward(h, 0, 10 * block)

    def far_experts(h):
        for hops in (3, 4):
            for way in ways_at(hops, h):
                crossing[h, hops, way].wait_recv()
        feed_forward(h, 10 * block, 16 * block)

    over_x = {}
    home = {}
    last_cross = {}

    def number_of(hops, way):
        if hops == 0:
            return 0
        if hops == 4:
            return 7
        return 1 + (hops - 1) * 2 + way

    def sum_cross(h, hops, way):
        over_x[h, hops, way] = send(
            place(parts, h, slot(1, way, hops), SPLIT),
            place(from_x, h, number_of(hops, way), 0, width - SPLIT),
            across,
        )

    def take_cross(h, hops, way):
        over_x[h, hops, way].wait_recv()
        add_blocks(h, slot(0, way, hops), SPLIT, width, [(from_x, number_of(hops, way), SPLIT)])

    def sum_hop(h, hops, way, col):
        stop = width if col == 0 else SPLIT
        landing = from_y if col == 0 else from_y_other
        home[h, hops, way, col] = send(
            place(parts, h, slot(col, way, hops), 0, stop),
            place(landing, h, (hops - 1) * 2 + way, 0, stop),
            homeward[way],
        )

    def take_other(h, hops, way):
        home[h, hops, way, 1].wait_recv()
        number = (hops - 1) * 2 + way
        add_blocks(h, slot(1, way, hops - 1), 0, SPLIT, [(from_y_other, number, 0)])

    def add_blocks(h, number, start, stop, terms):
        to_rows = slice(number * block, (number + 1) * block)
        for lo in range(start, stop, 512):
            total = parts[h, to_rows, lo : lo + 512].astype(jnp.float32)
            for ref, ref_number, offset in terms:
                ref_rows = slice(ref_number * block, (ref_number + 1) * block)
                if lo >= offset:
                    total = total + ref[
                        h, ref_rows, lo - offset : lo - offset + 512
                    ].astype(jnp.float32)
            parts[h, to_rows, lo : lo + 512] = total.astype(jnp.bfloat16)

    def sum_start(h):
        for hops in (4, 3, 2, 1):
            for way in ways_at(hops, h)[:: 1 if h else -1]:
                sum_cross(h, hops, way)
        sum_cross(h, 0, 0)
        sum_hop(h, 4, h, 1)
        sum_hop(h, 3, 1 - h, 1)
        take_cross(h, 4, h)
        sum_hop(h, 4, h, 0)
        take_cross(h, 3, 1 - h)
        sum_hop(h, 3, 1 - h, 0)

    def sum_step(h, hops):
        going_on = (0, 1) if hops < 3 else (h,)
        for way in going_on:
            take_other(h, hops + 1, way)
            sum_hop(h, hops, way, 1)
        for way in going_on:
            over_x[h, hops, way].wait_recv()
            home[h, hops + 1, way, 0].wait_recv()
            terms = [(from_y, hops * 2 + way, 0), (from_x, number_of(hops, way), SPLIT)]
            add_blocks(h, slot(0, way, hops), 0, width, terms)
            sum_hop(h, hops, way, 0)

    def sum_end(h):
        for way in (0, 1):
            home[h, 1, way, 1].wait_recv()
        add_blocks(h, 1, 0, SPLIT, [(from_y_other, 0, 0), (from_y_other, 1, 0)])
        last_cross[h] = send(place(parts, h, 1, 0, SPLIT), place(from_x_last, h, 0, 0, SPLIT), across)
        over_x[h, 0, 0].wait_recv()
        for way in (0, 1):
            home[h, 1, way, 0].wait_recv()
        add_blocks(h, 0, 0, width, [(from_y, 0, 0), (from_y, 1, 0), (from_x, 0, SPLIT)])

    steps = new_ref.shape[1]
    fresh_even[...] = jnp.zeros(fresh_even.shape, fresh_even.dtype)
    fresh_odd[...] = jnp.zeros(fresh_odd.shape, fresh_odd.dtype)
    for r in range(fresh_even.shape[0]):
        fresh_even[r, 0:steps, 0:lat] = new_ref[r]
        fresh_odd[r, 0:steps, ROPE : ROPE + lat] = new_ref[r]
    for ref in (cache.at[0], cache.at[1], handed):
        ref[0:ROPE, :] = jnp.zeros((ROPE, 2 * half), jnp.bfloat16)
        ref[ROPE + lat :, :] = jnp.zeros((ROPE, 2 * half), jnp.bfloat16)
    reqs = cache.shape[0]
    kv = lat - ROPE
    window = lat + ROPE
    pairs = query.shape[2] // (2 * lat)
    device = (section * experts + expert) * (2 * RING) + dp
    source = source_ref[0, dp]
    source_across = source_ref[0, (1 - x) * RING + y]

    def attend(r, keys, length):
        for p in range(pairs):
            lo = 2 * lat * p
            even[steps * p : steps * (p + 1), :] = query[r, :, lo : lo + window]
            odd[steps * p : steps * (p + 1), :] = query[r, :, lo + lat - ROPE : lo + 2 * lat]
        over_last = (((1,), (1,)), ((), ()))
        scores = softmax_scale * jnp.concatenate(
            [
                jnp.dot(even[...], keys[ROPE:, :], preferred_element_type=jnp.float32),
                jnp.dot(odd[...], keys[0:window, :], preferred_element_type=jnp.float32),
            ],
            axis=0,
        )
        new_scores = softmax_scale * jnp.concatenate(
            [
                lax.dot_general(
                    queries[...], new[r], over_last, preferred_element_type=jnp.float32
                )
                for queries, new in ((even, fresh_even), (odd, fresh_odd))
            ],
            axis=0,
        )
        lane = lax.broadcasted_iota(jnp.int32, scores.shape, 1)
        new_lane = lax.broadcasted_iota(jnp.int32, new_scores.shape, 1)
        step = lax.rem(lax.broadcasted_iota(jnp.int32, new_scores.shape, 0), steps)
        scores = jnp.where(lane < length, scores, -jnp.inf)
        new_scores = jnp.where(new_lane <= step, new_scores, -jnp.inf)
        top = jnp.maximum(
            jnp.max(scores, axis=1, keepdims=True), jnp.max(new_scores, axis=1, keepdims=True)
        )
        weights = jnp.exp(scores - top)
        new_weights = jnp.exp(new_scores - top)
        total = jnp.sum(weights, axis=1, keepdims=True) + jnp.sum(
            new_weights, axis=1, keepdims=True
        )
        context[...] = (
            lax.dot_general(
                (weights / total).astype(jnp.bfloat16),
                keys[ROPE : ROPE + kv, :],
                over_last,
                preferred_element_type=jnp.float32,
            )
            + jnp.dot(
                (new_weights / total).astype(jnp.bfloat16),
                fresh_even[r, :, 0:kv],
                preferred_element_type=jnp.float32,
            )
        ).astype(jnp.bfloat16)
        for p in range(pairs):
            for parity in (0, 1):
                first = (parity * pairs + p) * steps
                lo = (2 * p + parity) * kv
                context_ref[r, :, lo : lo + kv] = context[first : first + steps, :]

    land(0)
    gather_start(0)
    land(1)
    gather_start(1)
    for load in loads:
        load.wait()
    gather_other(0)
    gather_other(1)
    for arrived in hand:
        arrived.wait_recv()
    hand = hand_hop(2)
    for hops in (1, 2):
        for h in (0, 1):
            gather_step(h, hops)
        attend(hops - 1, cache.at[hops - 1], len_ref[device * reqs + hops - 1])
    for h in (0, 1):
        gather_step(h, 3)
        near_experts(h)
    for h in (0, 1):
        gather_step(h, 4)
    for arrived in hand:
        arrived.wait_recv()
    hand = hand_hop(3)
    for h in (0, 1):
        far_experts(h)
        sum_start(h)
    for h in (0, 1):
        sum_step(h, 3)
    for arrived in hand:
        arrived.wait_recv()
    hand = hand_hop(4)
    for h in (0, 1):
        sum_step(h, 2)
    for arrived in hand:
        arrived.wait_recv()
    pick_out[...] = held[lax.rem(lax.rem(source_across, RING) - y + RING, RING)]
    pick_pair[0] = held[lax.rem(lax.rem(source, RING) - y + RING, RING)]
    swap = send(pick_out, pick_pair.at[1], across)
    for h in (0, 1):
        sum_step(h, 1)
    for h in (0, 1):
        sum_end(h)

    back = {}
    for h in (0, 1):
        last_cross[h].wait_recv()
        add_blocks(h, 0, 0, SPLIT, [(from_x_last, 0, 0)])
        for i, j in enumerate(order[h]):
            if j == 0:
                picked_rows[0:CAP, :] = parts[h, CAP * i : CAP * (i + 1), :]
            else:
                going[j] = parts[h, CAP * i : CAP * (i + 1), :]
                back[j] = send(
                    going.at[j], coming.at[j], {"expert": lax.rem(expert + experts - j, experts)}
                )

    swap.wait_recv()
    picked[...] = pick_pair[jnp.where(source // RING == x, 0, 1)]
    second_cross = copy_to(picked, handed_half, other_section)
    handed[ROPE : ROPE + lat, half : 2 * half] = picked[...]

    @pl.when(section == 0)
    def _():
        second_cross.start()
        handed[ROPE : ROPE + lat, 0:half] = picked[...]

    @pl.when(section == 1)
    def _():
        second_cross.wait_recv()
        handed[ROPE : ROPE + lat, 0:half] = handed_half[...]

    source_row = (expert * 2 * RING + source) * reqs + hand_slot_ref[0, dp]
    attend(reqs, handed, jnp.where(section == 1, len_ref[source_row], 0))

    for j in range(1, experts):
        back[j].wait_recv()
        picked_rows[CAP * j : CAP * (j + 1), :] = coming[j]
    moe_ref[...] = lax.dot_general(
        mixing,
        picked_rows[...].astype(jnp.float32),
        (((0,), (0,)), ((), ())),
        precision=highest,
    ).astype(jnp.bfloat16)

    for copy in sent:
        copy.wait_send()

    @pl.when(section == 0)
    def _():
        first_cross.wait_send()
        second_cross.wait_send()


def shards(
    tokens,
    route_ids,
    route_weight,
    gate_weight,
    up_weight,
    down_weight,
    latent_cache,
    cache_len,
    hand_source,
    hand_slot,
    query_latent,
    new_latent,
):
    tok_rows, width = tokens.shape
    experts = lax.axis_size("expert")
    slot_count, step_count, _ = query_latent.shape
    requests, max_len, lat = latent_cache.shape
    lane_rows = experts * CAP
    half = max_len // 2
    kv = lat - ROPE
    query_rows = query_latent.shape[1] * query_latent.shape[2] // lat
    bf16 = jnp.bfloat16
    smem = pl.BlockSpec(memory_space=pltpu.SMEM)
    vmem = pl.BlockSpec(memory_space=pltpu.VMEM)
    anywhere = pl.BlockSpec(memory_space=pl.ANY)
    return pl.pallas_call(
        exchange,
        out_shape=(
            jax.ShapeDtypeStruct((tok_rows, width), bf16),
            jax.ShapeDtypeStruct((slot_count, step_count, query_rows // step_count * kv), bf16),
        ),
        in_specs=[smem] * 3 + [vmem] * 4 + [anywhere] * 5,
        out_specs=(vmem, vmem),
        scratch_shapes=[
            pltpu.VMEM((lane_rows, width), bf16),
            pltpu.VMEM((experts, CAP, width), bf16),
            pltpu.VMEM((experts, CAP, width), bf16),
            pltpu.VMEM((2, 8 * lane_rows, width), bf16),
            pltpu.VMEM((2, 8 * lane_rows, width), bf16),
            pltpu.VMEM((2, 4 * lane_rows, width), bf16),
            pltpu.VMEM((2, 4 * lane_rows, SPLIT), bf16),
            pltpu.VMEM((2, 4 * lane_rows, width - SPLIT), bf16),
            pltpu.VMEM((2, lane_rows // 2, SPLIT), bf16),
            pltpu.VMEM((experts, CAP, width), bf16),
            pltpu.VMEM((experts, CAP, width), bf16),
            pltpu.VMEM((requests, lat + 2 * ROPE, max_len), bf16),
            pltpu.VMEM(query_latent.shape, bf16),
            pltpu.VMEM((slot_count, 16, lat + ROPE), bf16),
            pltpu.VMEM((slot_count, 16, lat + ROPE), bf16),
            pltpu.VMEM((query_rows // 2, lat + ROPE), bf16),
            pltpu.VMEM((query_rows // 2, lat + ROPE), bf16),
            pltpu.VMEM((query_rows, kv), bf16),
            pltpu.VMEM((lat, max_len), bf16),
            pltpu.VMEM((RING, lat, half), bf16),
            pltpu.VMEM((2, lat, half), bf16),
            pltpu.VMEM((lat, half), bf16),
            pltpu.VMEM((lat, half), bf16),
            pltpu.VMEM((lat, half), bf16),
            pltpu.VMEM((lat + 2 * ROPE, max_len), bf16),
            pltpu.VMEM((width, 256), bf16),
            pltpu.VMEM((128, width), bf16),
            pltpu.SemaphoreType.DMA((160,)),
            pltpu.SemaphoreType.DMA((160,)),
            pltpu.SemaphoreType.DMA((5,)),
        ],
        compiler_params=pltpu.CompilerParams(
            collective_id=0, has_side_effects=True, vmem_limit_bytes=62 * 1024 * 1024
        ),
    )(
        hand_source,
        hand_slot,
        cache_len,
        tokens,
        route_ids.T,
        route_weight.T,
        new_latent,
        jnp.swapaxes(latent_cache, 1, 2),
        query_latent,
        gate_weight[0],
        up_weight[0],
        down_weight[0],
    )


def solution(mesh):
    return jax.shard_map(
        shards,
        mesh=mesh,
        in_specs=(
            P(("section", "expert", "dp"), None),
            P(("section", "expert", "dp"), None),
            P(("section", "expert", "dp"), None),
            P(("section", "expert"), None, "dp"),
            P(("section", "expert"), None, "dp"),
            P(("section", "expert"), "dp", None),
            P(("section", "expert", "dp"), None, None),
            P(),
            P("expert", None),
            P("expert", None),
            P(("section", "expert", "dp"), None, None),
            P(("section", "expert", "dp"), None, None),
        ),
        out_specs=(
            P(("section", "expert", "dp"), None),
            P(("section", "expert", "dp"), None, None),
        ),
        check_vma=False,
    )
```

```python
import jax
import jax.numpy as jnp
from jax import lax
from jax.experimental import pallas as pl
from jax.experimental.pallas import tpu as pltpu
from jax.sharding import PartitionSpec as P

CAP = 2
ROPE = 64
RING = 8
SPLIT = 1280
MESH = pl.DeviceIdType.MESH

softmax_scale = 192.0 ** (-0.5)
highest = lax.Precision.HIGHEST


def slot(col, way, hops):
    if hops == 0:
        return col
    if hops == 4:
        return 14 + col
    return 2 + (hops - 1) * 4 + col * 2 + way


def exchange(
    source_ref,
    hand_slot_ref,
    len_ref,
    tokens_ref,
    ids_ref,
    weight_ref,
    new_ref,
    cache_ref,
    query_ref,
    gate_ref,
    up_ref,
    down_ref,
    moe_ref,
    context_ref,
    picked_rows,
    leaving,
    landed,
    rows,
    parts,
    from_y,
    from_y_other,
    from_x,
    from_x_last,
    going,
    coming,
    cache,
    query,
    tokens,
    fresh,
    fresh_even,
    fresh_odd,
    even,
    odd,
    context,
    chosen,
    held,
    pick_pair,
    pick_out,
    picked,
    handed_half,
    handed,
    gate_up,
    down,
    send_sem,
    recv_sem,
    local_sem,
):
    width = rows.shape[2]
    section = lax.axis_index("section")
    expert = lax.axis_index("expert")
    dp = lax.axis_index("dp")
    experts = leaving.shape[0]
    x = dp // RING
    y = lax.rem(dp, RING)
    y_next = {"dp": x * RING + lax.rem(y + 1, RING)}
    y_back = {"dp": x * RING + lax.rem(y + RING - 1, RING)}
    across = {"dp": (1 - x) * RING + y}
    other_section = {"section": 1 - section, "dp": (1 - x) * RING + y}
    ways = (y_next, y_back)
    homeward = (y_back, y_next)

    loads = [
        pltpu.make_async_copy(gate_ref, gate_up.at[:, 0:128], local_sem.at[0]),
        pltpu.make_async_copy(up_ref, gate_up.at[:, 128:256], local_sem.at[1]),
        pltpu.make_async_copy(down_ref, down, local_sem.at[2]),
        pltpu.make_async_copy(query_ref, query, local_sem.at[3]),
        pltpu.make_async_copy(new_ref, fresh, local_sem.at[6]),
    ]
    cache_load = pltpu.make_async_copy(
        cache_ref, cache.at[:, ROPE : ROPE + cache_ref.shape[1]], local_sem.at[4]
    )
    token_load = pltpu.make_async_copy(tokens_ref, tokens, local_sem.at[5])
    token_load.start()
    cache_load.start()
    for load in loads:
        load.start()

    barrier = pltpu.get_barrier_semaphore()
    for peer in (y_next, y_back, across, other_section):
        pl.semaphore_signal(barrier, inc=1, device_id=peer, device_id_type=MESH)
    for j in range(1, experts):
        peer = {"expert": lax.rem(expert + j, experts)}
        pl.semaphore_signal(barrier, inc=1, device_id=peer, device_id_type=MESH)

    choices, tok_rows = ids_ref.shape
    slots = experts * CAP
    relative = lax.rem(ids_ref[...] - expert + experts, experts)
    slot_row = lax.broadcasted_iota(jnp.int32, (slots, tok_rows), 0)
    hits = jnp.zeros((slots, tok_rows), jnp.float32)
    mixing = jnp.zeros((slots, tok_rows), jnp.float32)
    for k in range(choices):
        hit = relative[k : k + 1, :] == slot_row // CAP
        hits = hits + jnp.where(hit, 1.0, 0.0)
        mixing = mixing + jnp.where(hit, weight_ref[k : k + 1, :], 0.0)
    token_row = lax.broadcasted_iota(jnp.int32, (tok_rows, tok_rows), 0)
    token_lane = lax.broadcasted_iota(jnp.int32, (tok_rows, tok_rows), 1)
    before = jnp.where(token_row < token_lane, 1.0, 0.0)
    earlier = jnp.dot(
        hits.astype(jnp.bfloat16), before.astype(jnp.bfloat16), preferred_element_type=jnp.float32
    )
    taken = jnp.where(earlier == lax.rem(slot_row, CAP).astype(jnp.float32), hits, 0.0)
    mixing = mixing * taken
    token_load.wait()
    picked_rows[...] = jnp.dot(
        taken.astype(jnp.bfloat16), tokens[...], preferred_element_type=jnp.float32
    ).astype(jnp.bfloat16)
    for j in range(1, experts):
        leaving[j] = picked_rows[CAP * j : CAP * (j + 1), :]
    count = [0]
    sent = []

    def copy_to(src, dst, device):
        number = count[0]
        count[0] += 1
        return pltpu.make_async_remote_copy(
            src_ref=src,
            dst_ref=dst,
            send_sem=send_sem.at[number],
            recv_sem=recv_sem.at[number],
            device_id=device,
            device_id_type=MESH,
        )

    def send(src, dst, device):
        copy = copy_to(src, dst, device)
        copy.start()
        sent.append(copy)
        return copy

    chosen_slot = 0
    for j in range(2 * RING):
        chosen_slot += jnp.where(source_ref[0, j] == dp, hand_slot_ref[0, j], 0)
    half = held.shape[2]
    lat = held.shape[1]
    cache_load.wait()
    chosen[...] = cache[chosen_slot, ROPE : ROPE + lat, :]
    first_cross = copy_to(chosen.at[:, half : 2 * half], held.at[0], other_section)
    hand = {}
    for hops in (1, 2, 3):
        hand[hops] = (
            copy_to(held.at[(RING - hops + 1) % RING], held.at[RING - hops], y_next),
            copy_to(held.at[hops - 1], held.at[hops], y_back),
        )
    hand[4] = (
        copy_to(held.at[RING - 3, 0 : lat // 2], held.at[4, 0 : lat // 2], y_next),
        copy_to(held.at[3, lat // 2 : lat], held.at[4, lat // 2 : lat], y_back),
    )

    def hand_start(hops):
        for copy in hand[hops]:
            copy.start()

    def hand_on(hops):
        for copy in hand[hops - 1]:
            copy.wait_recv()
        if hops in hand:
            hand_start(hops)

    @pl.when(section == 0)
    def _():
        held[0] = chosen[:, 0:half]

    pl.semaphore_wait(barrier, 4 + experts - 1)

    dispatch = {}
    for j in (1, 15, 2, 14, 3, 13, 4, 12, 5, 11, 6, 10, 7, 9, 8):
        peer = {"expert": lax.rem(expert + j, experts)}
        dispatch[j] = send(leaving.at[j], landed.at[j], peer)

    @pl.when(section == 0)
    def _():
        hand_start(1)
        first_cross.start()

    order = ((0, 1, 15, 2, 14, 3, 13, 4), (12, 5, 11, 6, 10, 7, 9, 8))
    block = rows.shape[1] // (2 * RING)

    def land(h):
        for i, j in enumerate(order[h]):
            if j == 0:
                rows[h, CAP * i : CAP * (i + 1), :] = picked_rows[0:CAP, :]
            else:
                dispatch[j].wait_recv()
                rows[h, CAP * i : CAP * (i + 1), :] = landed[j]

    def place(ref, h, number, start=0, stop=None):
        stop = width if stop is None else stop
        return ref.at[h, number * block : (number + 1) * block, start:stop]

    def ways_at(hops, h):
        return (0, 1) if hops < 4 else (h,)

    own = {}
    other = {}
    crossing = {}

    def own_hop(h, hops, way):
        own[h, hops, way] = send(
            place(rows, h, slot(0, way, hops - 1)), place(rows, h, slot(0, way, hops)), ways[way]
        )

    def other_hop(h, hops, way):
        other[h, hops, way] = send(
            place(rows, h, slot(1, way, hops - 1), 0, SPLIT),
            place(rows, h, slot(1, way, hops), 0, SPLIT),
            ways[way],
        )

    def cross_hop(h, hops, way):
        start = 0 if hops == 0 else SPLIT
        crossing[h, hops, way] = send(
            place(rows, h, slot(0, way, hops), start),
            place(rows, h, slot(1, way, hops), start),
            across,
        )

    def gather_start(h):
        cross_hop(h, 0, 0)
        for way in (0, 1):
            own_hop(h, 1, way)

    def gather_other(h):
        crossing[h, 0, 0].wait_recv()
        for way in (0, 1):
            other_hop(h, 1, way)

    def gather_step(h, hops):
        for way in ways_at(hops, h):
            own[h, hops, way].wait_recv()
            if hops < 4 and way in ways_at(hops + 1, h):
                own_hop(h, hops + 1, way)
            cross_hop(h, hops, way)
        for way in ways_at(hops, h):
            other[h, hops, way].wait_recv()
            if hops < 4 and way in ways_at(hops + 1, h):
                other_hop(h, hops + 1, way)

    def feed_forward(h, first, last):
        chunk = 512
        acc = jnp.dot(rows[h, first:last, :], gate_up[...], preferred_element_type=jnp.float32)
        gate = acc[:, 0:128]
        hidden = (gate / (1.0 + jnp.exp(-gate)) * acc[:, 128:256]).astype(jnp.bfloat16)
        for start in range(0, width, chunk):
            parts[h, first:last, start : start + chunk] = jnp.dot(
                hidden, down[:, start : start + chunk], preferred_element_type=jnp.float32
            ).astype(jnp.bfloat16)

    def near_experts(h):
        for hops in (1, 2):
            for way in (0, 1):
                crossing[h, hops, way].wait_recv()
        feed_forward(h, 0, 10 * block)

    def far_experts(h):
        for hops in (3, 4):
            for way in ways_at(hops, h):
                crossing[h, hops, way].wait_recv()
        feed_forward(h, 10 * block, 16 * block)

    over_x = {}
    home = {}
    last_cross = {}

    def number_of(hops, way):
        if hops == 0:
            return 0
        if hops == 4:
            return 7
        return 1 + (hops - 1) * 2 + way

    def sum_cross(h, hops, way):
        over_x[h, hops, way] = send(
            place(parts, h, slot(1, way, hops), SPLIT),
            place(from_x, h, number_of(hops, way), 0, width - SPLIT),
            across,
        )

    def take_cross(h, hops, way):
        over_x[h, hops, way].wait_recv()
        add_blocks(h, slot(0, way, hops), SPLIT, width, [(from_x, number_of(hops, way), SPLIT)])

    def sum_hop(h, hops, way, col):
        stop = width if col == 0 else SPLIT
        landing = from_y if col == 0 else from_y_other
        home[h, hops, way, col] = send(
            place(parts, h, slot(col, way, hops), 0, stop),
            place(landing, h, (hops - 1) * 2 + way, 0, stop),
            homeward[way],
        )

    def take_other(h, hops, way):
        home[h, hops, way, 1].wait_recv()
        number = (hops - 1) * 2 + way
        add_blocks(h, slot(1, way, hops - 1), 0, SPLIT, [(from_y_other, number, 0)])

    def add_blocks(h, number, start, stop, terms):
        to_rows = slice(number * block, (number + 1) * block)
        for lo in range(start, stop, 256):
            total = parts[h, to_rows, lo : lo + 256].astype(jnp.float32)
            for ref, ref_number, offset in terms:
                ref_rows = slice(ref_number * block, (ref_number + 1) * block)
                if lo >= offset:
                    total = total + ref[
                        h, ref_rows, lo - offset : lo - offset + 256
                    ].astype(jnp.float32)
            parts[h, to_rows, lo : lo + 256] = total.astype(jnp.bfloat16)

    def sum_start(h):
        for hops in (4, 3, 2, 1):
            for way in ways_at(hops, h)[:: 1 if h else -1]:
                sum_cross(h, hops, way)
        sum_cross(h, 0, 0)
        sum_hop(h, 4, h, 1)
        sum_hop(h, 3, 1 - h, 1)
        take_cross(h, 4, h)
        sum_hop(h, 4, h, 0)
        take_cross(h, 3, 1 - h)
        sum_hop(h, 3, 1 - h, 0)

    def sum_step(h, hops):
        going_on = (0, 1) if hops < 3 else (h,)
        for way in going_on:
            take_other(h, hops + 1, way)
            sum_hop(h, hops, way, 1)
        for way in going_on:
            over_x[h, hops, way].wait_recv()
            home[h, hops + 1, way, 0].wait_recv()
            terms = [(from_y, hops * 2 + way, 0), (from_x, number_of(hops, way), SPLIT)]
            add_blocks(h, slot(0, way, hops), 0, width, terms)
            sum_hop(h, hops, way, 0)

    def sum_end(h):
        for way in (0, 1):
            home[h, 1, way, 1].wait_recv()
        add_blocks(h, 1, 0, SPLIT, [(from_y_other, 0, 0), (from_y_other, 1, 0)])
        last_cross[h] = send(place(parts, h, 1, 0, SPLIT), place(from_x_last, h, 0, 0, SPLIT), across)
        over_x[h, 0, 0].wait_recv()
        for way in (0, 1):
            home[h, 1, way, 0].wait_recv()
        add_blocks(h, 0, 0, width, [(from_y, 0, 0), (from_y, 1, 0), (from_x, 0, SPLIT)])

    steps = fresh.shape[1]

    def keep_fresh():
        fresh_even[...] = jnp.zeros(fresh_even.shape, fresh_even.dtype)
        fresh_odd[...] = jnp.zeros(fresh_odd.shape, fresh_odd.dtype)
        for r in range(fresh_even.shape[0]):
            fresh_even[r, 0:steps, 0:lat] = fresh[r]
            fresh_odd[r, 0:steps, ROPE : ROPE + lat] = fresh[r]
        for ref in (cache.at[0], cache.at[1], handed):
            ref[0:ROPE, :] = jnp.zeros((ROPE, 2 * half), jnp.bfloat16)
            ref[ROPE + lat :, :] = jnp.zeros((ROPE, 2 * half), jnp.bfloat16)

    reqs = cache.shape[0]
    kv = lat - ROPE
    window = lat + ROPE
    pairs = query.shape[2] // (2 * lat)
    device = (section * experts + expert) * (2 * RING) + dp

    def attend(r, keys, length):
        for p in range(pairs):
            lo = 2 * lat * p
            even[steps * p : steps * (p + 1), :] = query[r, :, lo : lo + window]
            odd[steps * p : steps * (p + 1), :] = query[r, :, lo + lat - ROPE : lo + 2 * lat]
        over_last = (((1,), (1,)), ((), ()))
        scores = softmax_scale * jnp.concatenate(
            [
                jnp.dot(even[...], keys[ROPE:, :], preferred_element_type=jnp.float32),
                jnp.dot(odd[...], keys[0:window, :], preferred_element_type=jnp.float32),
            ],
            axis=0,
        )
        new_scores = softmax_scale * jnp.concatenate(
            [
                lax.dot_general(
                    queries[...], new[r], over_last, preferred_element_type=jnp.float32
                )
                for queries, new in ((even, fresh_even), (odd, fresh_odd))
            ],
            axis=0,
        )
        lane = lax.broadcasted_iota(jnp.int32, scores.shape, 1)
        new_lane = lax.broadcasted_iota(jnp.int32, new_scores.shape, 1)
        step = lax.rem(lax.broadcasted_iota(jnp.int32, new_scores.shape, 0), steps)
        scores = jnp.where(lane < length, scores, -jnp.inf)
        new_scores = jnp.where(new_lane <= step, new_scores, -jnp.inf)
        top = jnp.maximum(
            jnp.max(scores, axis=1, keepdims=True), jnp.max(new_scores, axis=1, keepdims=True)
        )
        weights = jnp.exp(scores - top)
        new_weights = jnp.exp(new_scores - top)
        total = jnp.sum(weights, axis=1, keepdims=True) + jnp.sum(
            new_weights, axis=1, keepdims=True
        )
        context[...] = (
            lax.dot_general(
                (weights / total).astype(jnp.bfloat16),
                keys[ROPE : ROPE + kv, :],
                over_last,
                preferred_element_type=jnp.float32,
            )
            + jnp.dot(
                (new_weights / total).astype(jnp.bfloat16),
                fresh_even[r, :, 0:kv],
                preferred_element_type=jnp.float32,
            )
        ).astype(jnp.bfloat16)
        for p in range(pairs):
            for parity in (0, 1):
                first = (parity * pairs + p) * steps
                lo = (2 * p + parity) * kv
                context_ref[r, :, lo : lo + kv] = context[first : first + steps, :]

    @pl.when(section == 0)
    def _():
        hand_on(2)

    land(0)
    gather_start(0)
    land(1)
    gather_start(1)
    for load in loads:
        load.wait()
    keep_fresh()
    gather_other(0)
    gather_other(1)

    @pl.when(section == 1)
    def _():
        first_cross.wait_recv()
        hand_start(1)

    for h in (0, 1):
        gather_step(h, 1)

    @pl.when(section == 1)
    def _():
        hand_on(2)

    attend(0, cache.at[0], len_ref[device * reqs])
    for h in (0, 1):
        gather_step(h, 2)
    hand_on(3)
    attend(1, cache.at[1], len_ref[device * reqs + 1])
    for h in (0, 1):
        gather_step(h, 3)
        near_experts(h)
    for h in (0, 1):
        gather_step(h, 4)
    hand_on(4)
    for h in (0, 1):
        far_experts(h)
        sum_start(h)
    for h in (0, 1):
        sum_step(h, 3)

    hand_on(5)
    reach = jnp.where(section == 1, x, 1 - x)
    mine = source_ref[0, reach * RING + y]
    others = source_ref[0, (1 - reach) * RING + y]
    pick_out[...] = held[lax.rem(lax.rem(others, RING) - y + RING, RING)]
    pick_pair[0] = held[lax.rem(lax.rem(mine, RING) - y + RING, RING)]
    swap = send(pick_out, pick_pair.at[1], across)
    for h in (0, 1):
        sum_step(h, 2)
    swap.wait_recv()
    picked[...] = pick_pair[jnp.where(mine // RING == reach, 1, 0)]
    second_cross = copy_to(picked, handed_half, other_section)
    handed[ROPE : ROPE + lat, half : 2 * half] = picked[...]

    @pl.when(section == 0)
    def _():
        second_cross.start()
        handed[ROPE : ROPE + lat, 0:half] = picked[...]

    sum_step(0, 1)
    sum_end(0)
    sum_step(1, 1)

    back = {}
    for h in (0, 1):
        if h == 1:
            sum_end(1)
        last_cross[h].wait_recv()
        add_blocks(h, 0, 0, SPLIT, [(from_x_last, 0, 0)])
        for i, j in enumerate(order[h]):
            if j == 0:
                picked_rows[0:CAP, :] = parts[h, CAP * i : CAP * (i + 1), :]
            else:
                going[j] = parts[h, CAP * i : CAP * (i + 1), :]
                back[j] = send(
                    going.at[j], coming.at[j], {"expert": lax.rem(expert + experts - j, experts)}
                )

    @pl.when(section == 1)
    def _():
        second_cross.wait_recv()
        handed[ROPE : ROPE + lat, 0:half] = handed_half[...]

    source = source_ref[0, dp]
    source_row = (expert * 2 * RING + source) * reqs + hand_slot_ref[0, dp]
    attend(reqs, handed, jnp.where(section == 1, len_ref[source_row], 0))

    for j in range(1, experts):
        back[j].wait_recv()
        picked_rows[CAP * j : CAP * (j + 1), :] = coming[j]
    moe_ref[...] = lax.dot_general(
        mixing,
        picked_rows[...].astype(jnp.float32),
        (((0,), (0,)), ((), ())),
        precision=highest,
    ).astype(jnp.bfloat16)

    for copy in sent:
        copy.wait_send()
    for hops in hand:
        for copy in hand[hops]:
            copy.wait_send()

    @pl.when(section == 0)
    def _():
        first_cross.wait_send()
        second_cross.wait_send()


def hand_out(moe_ref, context_ref, moe_out_ref, context_out_ref, sem):
    slots = context_ref.shape[0]
    copies = [pltpu.make_async_copy(moe_ref, moe_out_ref, sem.at[slots])]
    for r in range(slots):
        copies.append(pltpu.make_async_copy(context_ref.at[r], context_out_ref.at[r], sem.at[r]))
    for copy in copies:
        copy.start()
    for copy in copies:
        copy.wait()


def shards(
    tokens,
    route_ids,
    route_weight,
    gate_weight,
    up_weight,
    down_weight,
    latent_cache,
    cache_len,
    hand_source,
    hand_slot,
    query_latent,
    new_latent,
):
    tok_rows, width = tokens.shape
    experts = lax.axis_size("expert")
    slot_count, step_count, _ = query_latent.shape
    requests, max_len, lat = latent_cache.shape
    lane_rows = experts * CAP
    half = max_len // 2
    kv = lat - ROPE
    query_rows = query_latent.shape[1] * query_latent.shape[2] // lat
    bf16 = jnp.bfloat16
    smem = pl.BlockSpec(memory_space=pltpu.SMEM)
    vmem = pl.BlockSpec(memory_space=pltpu.VMEM)
    anywhere = pl.BlockSpec(memory_space=pl.ANY)
    results = pl.pallas_call(
        exchange,
        out_shape=(
            jax.ShapeDtypeStruct((tok_rows, width), bf16),
            jax.ShapeDtypeStruct((slot_count, step_count, query_rows // step_count * kv), bf16),
        ),
        in_specs=[smem] * 3 + [anywhere] + [vmem] * 2 + [anywhere] * 6,
        out_specs=(vmem, vmem),
        scratch_shapes=[
            pltpu.VMEM((lane_rows, width), bf16),
            pltpu.VMEM((experts, CAP, width), bf16),
            pltpu.VMEM((experts, CAP, width), bf16),
            pltpu.VMEM((2, 8 * lane_rows, width), bf16),
            pltpu.VMEM((2, 8 * lane_rows, width), bf16),
            pltpu.VMEM((2, 4 * lane_rows, width), bf16),
            pltpu.VMEM((2, 4 * lane_rows, SPLIT), bf16),
            pltpu.VMEM((2, 4 * lane_rows, width - SPLIT), bf16),
            pltpu.VMEM((2, lane_rows // 2, SPLIT), bf16),
            pltpu.VMEM((experts, CAP, width), bf16),
            pltpu.VMEM((experts, CAP, width), bf16),
            pltpu.VMEM((requests, lat + 2 * ROPE, max_len), bf16),
            pltpu.VMEM(query_latent.shape, bf16),
            pltpu.VMEM(tokens.shape, bf16),
            pltpu.VMEM(new_latent.shape, bf16),
            pltpu.VMEM((slot_count, 16, lat + ROPE), bf16),
            pltpu.VMEM((slot_count, 16, lat + ROPE), bf16),
            pltpu.VMEM((query_rows // 2, lat + ROPE), bf16),
            pltpu.VMEM((query_rows // 2, lat + ROPE), bf16),
            pltpu.VMEM((query_rows, kv), bf16),
            pltpu.VMEM((lat, max_len), bf16),
            pltpu.VMEM((RING, lat, half), bf16),
            pltpu.VMEM((2, lat, half), bf16),
            pltpu.VMEM((lat, half), bf16),
            pltpu.VMEM((lat, half), bf16),
            pltpu.VMEM((lat, half), bf16),
            pltpu.VMEM((lat + 2 * ROPE, max_len), bf16),
            pltpu.VMEM((width, 256), bf16),
            pltpu.VMEM((128, width), bf16),
            pltpu.SemaphoreType.DMA((160,)),
            pltpu.SemaphoreType.DMA((160,)),
            pltpu.SemaphoreType.DMA((7,)),
        ],
        compiler_params=pltpu.CompilerParams(
            collective_id=0, has_side_effects=True, vmem_limit_bytes=62 * 1024 * 1024
        ),
    )(
        hand_source,
        hand_slot,
        cache_len,
        tokens,
        route_ids.T,
        route_weight.T,
        new_latent,
        jnp.swapaxes(latent_cache, 1, 2),
        query_latent,
        gate_weight[0],
        up_weight[0],
        down_weight[0],
    )
    return pl.pallas_call(
        hand_out,
        out_shape=tuple(jax.ShapeDtypeStruct(result.shape, bf16) for result in results),
        in_specs=[anywhere] * 2,
        out_specs=(anywhere, anywhere),
        scratch_shapes=[pltpu.SemaphoreType.DMA((slot_count + 1,))],
        compiler_params=pltpu.CompilerParams(vmem_limit_bytes=62 * 1024 * 1024),
    )(*results)


def solution(mesh):
    return jax.shard_map(
        shards,
        mesh=mesh,
        in_specs=(
            P(("section", "expert", "dp"), None),
            P(("section", "expert", "dp"), None),
            P(("section", "expert", "dp"), None),
            P(("section", "expert"), None, "dp"),
            P(("section", "expert"), None, "dp"),
            P(("section", "expert"), "dp", None),
            P(("section", "expert", "dp"), None, None),
            P(),
            P("expert", None),
            P("expert", None),
            P(("section", "expert", "dp"), None, None),
            P(("section", "expert", "dp"), None, None),
        ),
        out_specs=(
            P(("section", "expert", "dp"), None),
            P(("section", "expert", "dp"), None, None),
        ),
        check_vma=False,
    )
```

```python
import jax
import jax.numpy as jnp
from jax import lax
from jax.experimental import pallas as pl
from jax.experimental.pallas import tpu as pltpu
from jax.sharding import PartitionSpec as P

CAP = 2
ROPE = 64
RING = 8
GATHER_SPLIT = 1024
SUM_SPLIT = 1792
MESH = pl.DeviceIdType.MESH

softmax_scale = 192.0 ** (-0.5)
highest = lax.Precision.HIGHEST


def slot(col, way, hops):
    if hops == 0:
        return col
    if hops == 4:
        return 14 + col
    return 2 + (hops - 1) * 4 + col * 2 + way


def exchange(
    source_ref,
    hand_slot_ref,
    len_ref,
    tokens_ref,
    ids_ref,
    weight_ref,
    new_ref,
    cache_ref,
    query_ref,
    gate_ref,
    up_ref,
    down_ref,
    moe_ref,
    context_ref,
    picked_rows,
    leaving,
    landed,
    rows,
    parts,
    from_y,
    from_y_other,
    from_x,
    from_x_last,
    going,
    coming,
    cache,
    query,
    tokens,
    fresh,
    fresh_even,
    fresh_odd,
    even,
    odd,
    context,
    chosen,
    held,
    pick_pair,
    pick_out,
    picked,
    handed_half,
    handed,
    gate_up,
    down,
    send_sem,
    recv_sem,
    local_sem,
):
    width = rows.shape[2]
    section = lax.axis_index("section")
    expert = lax.axis_index("expert")
    dp = lax.axis_index("dp")
    experts = leaving.shape[0]
    x = dp // RING
    y = lax.rem(dp, RING)
    y_next = {"dp": x * RING + lax.rem(y + 1, RING)}
    y_back = {"dp": x * RING + lax.rem(y + RING - 1, RING)}
    across = {"dp": (1 - x) * RING + y}
    other_section = {"section": 1 - section, "dp": (1 - x) * RING + y}
    ways = (y_next, y_back)
    homeward = (y_back, y_next)

    loads = [
        pltpu.make_async_copy(gate_ref, gate_up.at[:, 0:128], local_sem.at[0]),
        pltpu.make_async_copy(up_ref, gate_up.at[:, 128:256], local_sem.at[1]),
        pltpu.make_async_copy(down_ref, down, local_sem.at[2]),
        pltpu.make_async_copy(query_ref, query, local_sem.at[3]),
        pltpu.make_async_copy(new_ref, fresh, local_sem.at[6]),
    ]
    cache_load = pltpu.make_async_copy(
        cache_ref, cache.at[:, ROPE : ROPE + cache_ref.shape[1]], local_sem.at[4]
    )
    token_load = pltpu.make_async_copy(tokens_ref, tokens, local_sem.at[5])
    token_load.start()
    cache_load.start()
    for load in loads:
        load.start()

    barrier = pltpu.get_barrier_semaphore()
    for peer in (y_next, y_back, across, other_section):
        pl.semaphore_signal(barrier, inc=1, device_id=peer, device_id_type=MESH)
    for j in range(1, experts):
        peer = {"expert": lax.rem(expert + j, experts)}
        pl.semaphore_signal(barrier, inc=1, device_id=peer, device_id_type=MESH)

    choices, tok_rows = ids_ref.shape
    slots = experts * CAP
    relative = lax.rem(ids_ref[...] - expert + experts, experts)
    slot_row = lax.broadcasted_iota(jnp.int32, (slots, tok_rows), 0)
    hits = jnp.zeros((slots, tok_rows), jnp.float32)
    mixing = jnp.zeros((slots, tok_rows), jnp.float32)
    for k in range(choices):
        hit = relative[k : k + 1, :] == slot_row // CAP
        hits = hits + jnp.where(hit, 1.0, 0.0)
        mixing = mixing + jnp.where(hit, weight_ref[k : k + 1, :], 0.0)
    token_row = lax.broadcasted_iota(jnp.int32, (tok_rows, tok_rows), 0)
    token_lane = lax.broadcasted_iota(jnp.int32, (tok_rows, tok_rows), 1)
    before = jnp.where(token_row < token_lane, 1.0, 0.0)
    earlier = jnp.dot(
        hits.astype(jnp.bfloat16), before.astype(jnp.bfloat16), preferred_element_type=jnp.float32
    )
    taken = jnp.where(earlier == lax.rem(slot_row, CAP).astype(jnp.float32), hits, 0.0)
    mixing = mixing * taken
    token_load.wait()
    picked_rows[...] = jnp.dot(
        taken.astype(jnp.bfloat16), tokens[...], preferred_element_type=jnp.float32
    ).astype(jnp.bfloat16)
    for j in range(1, experts):
        leaving[j] = picked_rows[CAP * j : CAP * (j + 1), :]
    count = [0]
    sent = []

    def copy_to(src, dst, device):
        number = count[0]
        count[0] += 1
        return pltpu.make_async_remote_copy(
            src_ref=src,
            dst_ref=dst,
            send_sem=send_sem.at[number],
            recv_sem=recv_sem.at[number],
            device_id=device,
            device_id_type=MESH,
        )

    def send(src, dst, device):
        copy = copy_to(src, dst, device)
        copy.start()
        sent.append(copy)
        return copy

    pl.semaphore_wait(barrier, 4 + experts - 1)

    dispatch = {}
    for j in (1, 15, 2, 14, 3, 13, 4, 12, 5, 11, 6, 10, 7, 9, 8):
        peer = {"expert": lax.rem(expert + j, experts)}
        dispatch[j] = send(leaving.at[j], landed.at[j], peer)

    chosen_slot = 0
    for j in range(2 * RING):
        chosen_slot += jnp.where(source_ref[0, j] == dp, hand_slot_ref[0, j], 0)
    half = held.shape[2]
    lat = held.shape[1]
    cache_load.wait()
    chosen[...] = cache[chosen_slot, ROPE : ROPE + lat, :]
    first_cross = copy_to(chosen.at[:, half : 2 * half], held.at[0], other_section)
    hand = {}
    for hops in (1, 2, 3):
        hand[hops] = (
            copy_to(held.at[(RING - hops + 1) % RING], held.at[RING - hops], y_next),
            copy_to(held.at[hops - 1], held.at[hops], y_back),
        )
    hand[4] = (
        copy_to(held.at[RING - 3, 0 : lat // 2], held.at[4, 0 : lat // 2], y_next),
        copy_to(held.at[3, lat // 2 : lat], held.at[4, lat // 2 : lat], y_back),
    )

    def hand_start(hops):
        for copy in hand[hops]:
            copy.start()

    def hand_on(hops):
        for copy in hand[hops - 1]:
            copy.wait_recv()
        if hops in hand:
            hand_start(hops)

    @pl.when(section == 0)
    def _():
        first_cross.start()
        held[0] = chosen[:, 0:half]
        hand_start(1)

    order = ((0, 1, 15, 2, 14, 3, 13, 4), (12, 5, 11, 6, 10, 7, 9, 8))
    block = rows.shape[1] // (2 * RING)

    def land(h):
        for i, j in enumerate(order[h]):
            if j == 0:
                rows[h, CAP * i : CAP * (i + 1), :] = picked_rows[0:CAP, :]
            else:
                dispatch[j].wait_recv()
                rows[h, CAP * i : CAP * (i + 1), :] = landed[j]

    def place(ref, h, number, start=0, stop=None):
        stop = width if stop is None else stop
        return ref.at[h, number * block : (number + 1) * block, start:stop]

    def ways_at(hops, h):
        return (0, 1) if hops < 4 else (h,)

    own = {}
    other = {}
    crossing = {}

    def own_hop(h, hops, way):
        own[h, hops, way] = send(
            place(rows, h, slot(0, way, hops - 1)), place(rows, h, slot(0, way, hops)), ways[way]
        )

    def other_hop(h, hops, way):
        other[h, hops, way] = send(
            place(rows, h, slot(1, way, hops - 1), 0, GATHER_SPLIT),
            place(rows, h, slot(1, way, hops), 0, GATHER_SPLIT),
            ways[way],
        )

    def cross_hop(h, hops, way):
        start = 0 if hops == 0 else GATHER_SPLIT
        crossing[h, hops, way] = send(
            place(rows, h, slot(0, way, hops), start),
            place(rows, h, slot(1, way, hops), start),
            across,
        )

    def gather_start(h):
        cross_hop(h, 0, 0)
        for way in (0, 1):
            own_hop(h, 1, way)

    def gather_other(h):
        crossing[h, 0, 0].wait_recv()
        for way in (0, 1):
            other_hop(h, 1, way)

    def gather_step(h, hops):
        for way in ways_at(hops, h):
            own[h, hops, way].wait_recv()
            if hops < 4 and way in ways_at(hops + 1, h):
                own_hop(h, hops + 1, way)
            cross_hop(h, hops, way)
        for way in ways_at(hops, h):
            other[h, hops, way].wait_recv()
            if hops < 4 and way in ways_at(hops + 1, h):
                other_hop(h, hops + 1, way)

    def feed_forward(h, first, last):
        chunk = 512
        acc = jnp.dot(rows[h, first:last, :], gate_up[...], preferred_element_type=jnp.float32)
        gate = acc[:, 0:128]
        hidden = (gate / (1.0 + jnp.exp(-gate)) * acc[:, 128:256]).astype(jnp.bfloat16)
        for start in range(0, width, chunk):
            parts[h, first:last, start : start + chunk] = jnp.dot(
                hidden, down[:, start : start + chunk], preferred_element_type=jnp.float32
            ).astype(jnp.bfloat16)

    def near_experts(h):
        for hops in (1, 2):
            for way in (0, 1):
                crossing[h, hops, way].wait_recv()
        feed_forward(h, 0, 10 * block)

    def far_experts(h):
        for hops in (3, 4):
            for way in ways_at(hops, h):
                crossing[h, hops, way].wait_recv()
        feed_forward(h, 10 * block, 16 * block)

    over_x = {}
    home = {}
    last_cross = {}

    def number_of(hops, way):
        if hops == 0:
            return 0
        if hops == 4:
            return 7
        return 1 + (hops - 1) * 2 + way

    def sum_cross(h, hops, way):
        over_x[h, hops, way] = send(
            place(parts, h, slot(1, way, hops), SUM_SPLIT),
            place(from_x, h, number_of(hops, way), 0, width - SUM_SPLIT),
            across,
        )

    def take_cross(h, hops, way):
        over_x[h, hops, way].wait_recv()
        add_blocks(h, slot(0, way, hops), SUM_SPLIT, width, [(from_x, number_of(hops, way), SUM_SPLIT)])

    def sum_hop(h, hops, way, col):
        stop = width if col == 0 else SUM_SPLIT
        landing = from_y if col == 0 else from_y_other
        home[h, hops, way, col] = send(
            place(parts, h, slot(col, way, hops), 0, stop),
            place(landing, h, (hops - 1) * 2 + way, 0, stop),
            homeward[way],
        )

    def take_other(h, hops, way):
        home[h, hops, way, 1].wait_recv()
        number = (hops - 1) * 2 + way
        add_blocks(h, slot(1, way, hops - 1), 0, SUM_SPLIT, [(from_y_other, number, 0)])

    def add_blocks(h, number, start, stop, terms):
        to_rows = slice(number * block, (number + 1) * block)
        for lo in range(start, stop, 256):
            total = parts[h, to_rows, lo : lo + 256].astype(jnp.float32)
            for ref, ref_number, offset in terms:
                ref_rows = slice(ref_number * block, (ref_number + 1) * block)
                if lo >= offset:
                    total = total + ref[
                        h, ref_rows, lo - offset : lo - offset + 256
                    ].astype(jnp.float32)
            parts[h, to_rows, lo : lo + 256] = total.astype(jnp.bfloat16)

    def sum_start(h):
        for hops in (4, 3, 2, 1):
            for way in ways_at(hops, h)[:: 1 if h else -1]:
                sum_cross(h, hops, way)
        sum_cross(h, 0, 0)
        sum_hop(h, 4, h, 1)
        sum_hop(h, 3, 1 - h, 1)
        take_cross(h, 4, h)
        sum_hop(h, 4, h, 0)
        take_cross(h, 3, 1 - h)
        sum_hop(h, 3, 1 - h, 0)

    def sum_step(h, hops):
        going_on = (0, 1) if hops < 3 else (h,)
        for way in going_on:
            take_other(h, hops + 1, way)
            sum_hop(h, hops, way, 1)
        for way in going_on:
            over_x[h, hops, way].wait_recv()
            home[h, hops + 1, way, 0].wait_recv()
            terms = [(from_y, hops * 2 + way, 0), (from_x, number_of(hops, way), SUM_SPLIT)]
            add_blocks(h, slot(0, way, hops), 0, width, terms)
            sum_hop(h, hops, way, 0)

    def sum_end(h):
        for way in (0, 1):
            home[h, 1, way, 1].wait_recv()
        add_blocks(h, 1, 0, SUM_SPLIT, [(from_y_other, 0, 0), (from_y_other, 1, 0)])
        last_cross[h] = send(place(parts, h, 1, 0, SUM_SPLIT), place(from_x_last, h, 0, 0, SUM_SPLIT), across)
        over_x[h, 0, 0].wait_recv()
        for way in (0, 1):
            home[h, 1, way, 0].wait_recv()
        add_blocks(h, 0, 0, width, [(from_y, 0, 0), (from_y, 1, 0), (from_x, 0, SUM_SPLIT)])

    steps = fresh.shape[1]

    def keep_fresh():
        fresh_even[...] = jnp.zeros(fresh_even.shape, fresh_even.dtype)
        fresh_odd[...] = jnp.zeros(fresh_odd.shape, fresh_odd.dtype)
        for r in range(fresh_even.shape[0]):
            fresh_even[r, 0:steps, 0:lat] = fresh[r]
            fresh_odd[r, 0:steps, ROPE : ROPE + lat] = fresh[r]
        for ref in (cache.at[0], cache.at[1], handed):
            ref[0:ROPE, :] = jnp.zeros((ROPE, 2 * half), jnp.bfloat16)
            ref[ROPE + lat :, :] = jnp.zeros((ROPE, 2 * half), jnp.bfloat16)

    reqs = cache.shape[0]
    kv = lat - ROPE
    window = lat + ROPE
    pairs = query.shape[2] // (2 * lat)
    device = (section * experts + expert) * (2 * RING) + dp

    def attend(r, keys, length):
        for p in range(pairs):
            lo = 2 * lat * p
            even[steps * p : steps * (p + 1), :] = query[r, :, lo : lo + window]
            odd[steps * p : steps * (p + 1), :] = query[r, :, lo + lat - ROPE : lo + 2 * lat]
        over_last = (((1,), (1,)), ((), ()))
        scores = softmax_scale * jnp.concatenate(
            [
                jnp.dot(even[...], keys[ROPE:, :], preferred_element_type=jnp.float32),
                jnp.dot(odd[...], keys[0:window, :], preferred_element_type=jnp.float32),
            ],
            axis=0,
        )
        new_scores = softmax_scale * jnp.concatenate(
            [
                lax.dot_general(
                    queries[...], new[r], over_last, preferred_element_type=jnp.float32
                )
                for queries, new in ((even, fresh_even), (odd, fresh_odd))
            ],
            axis=0,
        )
        lane = lax.broadcasted_iota(jnp.int32, scores.shape, 1)
        new_lane = lax.broadcasted_iota(jnp.int32, new_scores.shape, 1)
        step = lax.rem(lax.broadcasted_iota(jnp.int32, new_scores.shape, 0), steps)
        scores = jnp.where(lane < length, scores, -jnp.inf)
        new_scores = jnp.where(new_lane <= step, new_scores, -jnp.inf)
        top = jnp.maximum(
            jnp.max(scores, axis=1, keepdims=True), jnp.max(new_scores, axis=1, keepdims=True)
        )
        weights = jnp.exp(scores - top)
        new_weights = jnp.exp(new_scores - top)
        total = jnp.sum(weights, axis=1, keepdims=True) + jnp.sum(
            new_weights, axis=1, keepdims=True
        )
        context[...] = (
            lax.dot_general(
                (weights / total).astype(jnp.bfloat16),
                keys[ROPE : ROPE + kv, :],
                over_last,
                preferred_element_type=jnp.float32,
            )
            + jnp.dot(
                (new_weights / total).astype(jnp.bfloat16),
                fresh_even[r, :, 0:kv],
                preferred_element_type=jnp.float32,
            )
        ).astype(jnp.bfloat16)
        for p in range(pairs):
            for parity in (0, 1):
                first = (parity * pairs + p) * steps
                lo = (2 * p + parity) * kv
                context_ref[r, :, lo : lo + kv] = context[first : first + steps, :]

    land(0)
    gather_start(0)
    land(1)
    gather_start(1)
    for load in loads:
        load.wait()
    keep_fresh()
    gather_other(0)
    gather_other(1)

    @pl.when(section == 1)
    def _():
        first_cross.wait_recv()
        hand_start(1)

    for h in (0, 1):
        gather_step(h, 1)
    hand_on(2)
    attend(0, cache.at[0], len_ref[device * reqs])
    for h in (0, 1):
        gather_step(h, 2)
    hand_on(3)
    attend(1, cache.at[1], len_ref[device * reqs + 1])
    for h in (0, 1):
        gather_step(h, 3)
        near_experts(h)
    hand_on(4)
    for h in (0, 1):
        gather_step(h, 4)

    hand_on(5)
    reach = jnp.where(section == 1, x, 1 - x)
    mine = source_ref[0, reach * RING + y]
    others = source_ref[0, (1 - reach) * RING + y]
    pick_out[...] = held[lax.rem(lax.rem(others, RING) - y + RING, RING)]
    swap = send(pick_out, pick_pair.at[1], across)
    pick_pair[0] = held[lax.rem(lax.rem(mine, RING) - y + RING, RING)]
    for h in (0, 1):
        far_experts(h)
        sum_start(h)
    swap.wait_recv()
    picked[...] = pick_pair[jnp.where(mine // RING == reach, 1, 0)]
    second_cross = copy_to(picked, handed_half, other_section)
    handed[ROPE : ROPE + lat, half : 2 * half] = picked[...]

    @pl.when(section == 0)
    def _():
        second_cross.start()
        handed[ROPE : ROPE + lat, 0:half] = picked[...]

    for hops in (3, 2, 1):
        for h in (0, 1):
            sum_step(h, hops)
    for h in (0, 1):
        sum_end(h)

    back = {}
    for h in (0, 1):
        last_cross[h].wait_recv()
        add_blocks(h, 0, 0, SUM_SPLIT, [(from_x_last, 0, 0)])
        for i, j in enumerate(order[h]):
            if j == 0:
                picked_rows[0:CAP, :] = parts[h, CAP * i : CAP * (i + 1), :]
            else:
                going[j] = parts[h, CAP * i : CAP * (i + 1), :]
                back[j] = send(
                    going.at[j], coming.at[j], {"expert": lax.rem(expert + experts - j, experts)}
                )

    @pl.when(section == 1)
    def _():
        second_cross.wait_recv()
        handed[ROPE : ROPE + lat, 0:half] = handed_half[...]

    source = source_ref[0, dp]
    source_row = (expert * 2 * RING + source) * reqs + hand_slot_ref[0, dp]
    attend(reqs, handed, jnp.where(section == 1, len_ref[source_row], 0))

    for j in range(1, experts):
        back[j].wait_recv()
        picked_rows[CAP * j : CAP * (j + 1), :] = coming[j]
    moe_ref[...] = lax.dot_general(
        mixing,
        picked_rows[...].astype(jnp.float32),
        (((0,), (0,)), ((), ())),
        precision=highest,
    ).astype(jnp.bfloat16)

    for copy in sent:
        copy.wait_send()
    for hops in hand:
        for copy in hand[hops]:
            copy.wait_send()

    @pl.when(section == 0)
    def _():
        first_cross.wait_send()
        second_cross.wait_send()


def shards(
    tokens,
    route_ids,
    route_weight,
    gate_weight,
    up_weight,
    down_weight,
    latent_cache,
    cache_len,
    hand_source,
    hand_slot,
    query_latent,
    new_latent,
):
    tok_rows, width = tokens.shape
    experts = lax.axis_size("expert")
    slot_count, step_count, _ = query_latent.shape
    requests, max_len, lat = latent_cache.shape
    lane_rows = experts * CAP
    half = max_len // 2
    kv = lat - ROPE
    query_rows = query_latent.shape[1] * query_latent.shape[2] // lat
    bf16 = jnp.bfloat16
    smem = pl.BlockSpec(memory_space=pltpu.SMEM)
    vmem = pl.BlockSpec(memory_space=pltpu.VMEM)
    anywhere = pl.BlockSpec(memory_space=pl.ANY)
    return pl.pallas_call(
        exchange,
        out_shape=(
            jax.ShapeDtypeStruct((tok_rows, width), bf16),
            jax.ShapeDtypeStruct((slot_count, step_count, query_rows // step_count * kv), bf16),
        ),
        in_specs=[smem] * 3 + [anywhere] + [vmem] * 2 + [anywhere] * 6,
        out_specs=(vmem, vmem),
        scratch_shapes=[
            pltpu.VMEM((lane_rows, width), bf16),
            pltpu.VMEM((experts, CAP, width), bf16),
            pltpu.VMEM((experts, CAP, width), bf16),
            pltpu.VMEM((2, 8 * lane_rows, width), bf16),
            pltpu.VMEM((2, 8 * lane_rows, width), bf16),
            pltpu.VMEM((2, 4 * lane_rows, width), bf16),
            pltpu.VMEM((2, 4 * lane_rows, SUM_SPLIT), bf16),
            pltpu.VMEM((2, 4 * lane_rows, width - SUM_SPLIT), bf16),
            pltpu.VMEM((2, lane_rows // 2, SUM_SPLIT), bf16),
            pltpu.VMEM((experts, CAP, width), bf16),
            pltpu.VMEM((experts, CAP, width), bf16),
            pltpu.VMEM((requests, lat + 2 * ROPE, max_len), bf16),
            pltpu.VMEM(query_latent.shape, bf16),
            pltpu.VMEM(tokens.shape, bf16),
            pltpu.VMEM(new_latent.shape, bf16),
            pltpu.VMEM((slot_count, 16, lat + ROPE), bf16),
            pltpu.VMEM((slot_count, 16, lat + ROPE), bf16),
            pltpu.VMEM((query_rows // 2, lat + ROPE), bf16),
            pltpu.VMEM((query_rows // 2, lat + ROPE), bf16),
            pltpu.VMEM((query_rows, kv), bf16),
            pltpu.VMEM((lat, max_len), bf16),
            pltpu.VMEM((RING, lat, half), bf16),
            pltpu.VMEM((2, lat, half), bf16),
            pltpu.VMEM((lat, half), bf16),
            pltpu.VMEM((lat, half), bf16),
            pltpu.VMEM((lat, half), bf16),
            pltpu.VMEM((lat + 2 * ROPE, max_len), bf16),
            pltpu.VMEM((width, 256), bf16),
            pltpu.VMEM((128, width), bf16),
            pltpu.SemaphoreType.DMA((160,)),
            pltpu.SemaphoreType.DMA((160,)),
            pltpu.SemaphoreType.DMA((7,)),
        ],
        compiler_params=pltpu.CompilerParams(
            collective_id=0, has_side_effects=True, vmem_limit_bytes=62 * 1024 * 1024
        ),
    )(
        hand_source,
        hand_slot,
        cache_len,
        tokens,
        route_ids.T,
        route_weight.T,
        new_latent,
        jnp.swapaxes(latent_cache, 1, 2),
        query_latent,
        gate_weight[0],
        up_weight[0],
        down_weight[0],
    )


def solution(mesh):
    return jax.shard_map(
        shards,
        mesh=mesh,
        in_specs=(
            P(("section", "expert", "dp"), None),
            P(("section", "expert", "dp"), None),
            P(("section", "expert", "dp"), None),
            P(("section", "expert"), None, "dp"),
            P(("section", "expert"), None, "dp"),
            P(("section", "expert"), "dp", None),
            P(("section", "expert", "dp"), None, None),
            P(),
            P("expert", None),
            P("expert", None),
            P(("section", "expert", "dp"), None, None),
            P(("section", "expert", "dp"), None, None),
        ),
        out_specs=(
            P(("section", "expert", "dp"), None),
            P(("section", "expert", "dp"), None, None),
        ),
        check_vma=False,
    )
```

```python
import jax
import jax.numpy as jnp
from jax import lax
from jax.experimental import pallas as pl
from jax.experimental.pallas import tpu as pltpu
from jax.sharding import PartitionSpec as P

CAP = 2
ROPE = 64
RING = 8
SPLIT = 1536
MESH = pl.DeviceIdType.MESH

softmax_scale = 192.0 ** (-0.5)
highest = lax.Precision.HIGHEST


def slot(col, way, hops):
    if hops == 0:
        return col
    if hops == 4:
        return 14 + col
    return 2 + (hops - 1) * 4 + col * 2 + way


def exchange(
    source_ref,
    hand_slot_ref,
    len_ref,
    tokens_ref,
    ids_ref,
    weight_ref,
    new_ref,
    cache_ref,
    query_ref,
    gate_ref,
    up_ref,
    down_ref,
    moe_ref,
    context_ref,
    picked_rows,
    leaving,
    landed,
    rows,
    parts,
    from_y,
    from_y_other,
    from_x,
    from_x_last,
    going,
    coming,
    cache,
    query,
    fresh_even,
    fresh_odd,
    even,
    odd,
    context,
    chosen,
    held,
    pick_pair,
    pick_out,
    picked,
    handed_half,
    handed,
    gate_up,
    down,
    send_sem,
    recv_sem,
    local_sem,
):
    width = rows.shape[2]
    section = lax.axis_index("section")
    expert = lax.axis_index("expert")
    dp = lax.axis_index("dp")
    experts = leaving.shape[0]
    x = dp // RING
    y = lax.rem(dp, RING)
    y_next = {"dp": x * RING + lax.rem(y + 1, RING)}
    y_back = {"dp": x * RING + lax.rem(y + RING - 1, RING)}
    across = {"dp": (1 - x) * RING + y}
    other_section = {"section": 1 - section}
    ways = (y_next, y_back)
    homeward = (y_back, y_next)

    loads = [
        pltpu.make_async_copy(gate_ref, gate_up.at[:, 0:128], local_sem.at[0]),
        pltpu.make_async_copy(up_ref, gate_up.at[:, 128:256], local_sem.at[1]),
        pltpu.make_async_copy(down_ref, down, local_sem.at[2]),
        pltpu.make_async_copy(query_ref, query, local_sem.at[3]),
    ]
    cache_load = pltpu.make_async_copy(
        cache_ref, cache.at[:, ROPE : ROPE + cache_ref.shape[1]], local_sem.at[4]
    )
    cache_load.start()
    for load in loads:
        load.start()

    barrier = pltpu.get_barrier_semaphore()
    for peer in (y_next, y_back, across, other_section):
        pl.semaphore_signal(barrier, inc=1, device_id=peer, device_id_type=MESH)
    for j in range(1, experts):
        peer = {"expert": lax.rem(expert + j, experts)}
        pl.semaphore_signal(barrier, inc=1, device_id=peer, device_id_type=MESH)

    choices, tok_rows = ids_ref.shape
    slots = experts * CAP
    relative = lax.rem(ids_ref[...] - expert + experts, experts)
    slot_row = lax.broadcasted_iota(jnp.int32, (slots, tok_rows), 0)
    hits = jnp.zeros((slots, tok_rows), jnp.float32)
    mixing = jnp.zeros((slots, tok_rows), jnp.float32)
    for k in range(choices):
        hit = relative[k : k + 1, :] == slot_row // CAP
        hits = hits + jnp.where(hit, 1.0, 0.0)
        mixing = mixing + jnp.where(hit, weight_ref[k : k + 1, :], 0.0)
    token_row = lax.broadcasted_iota(jnp.int32, (tok_rows, tok_rows), 0)
    token_lane = lax.broadcasted_iota(jnp.int32, (tok_rows, tok_rows), 1)
    before = jnp.where(token_row < token_lane, 1.0, 0.0)
    earlier = jnp.dot(
        hits.astype(jnp.bfloat16), before.astype(jnp.bfloat16), preferred_element_type=jnp.float32
    )
    taken = jnp.where(earlier == lax.rem(slot_row, CAP).astype(jnp.float32), hits, 0.0)
    mixing = mixing * taken
    picked_rows[...] = jnp.dot(
        taken.astype(jnp.bfloat16), tokens_ref[...], preferred_element_type=jnp.float32
    ).astype(jnp.bfloat16)
    for j in range(1, experts):
        leaving[j] = picked_rows[CAP * j : CAP * (j + 1), :]
    pl.semaphore_wait(barrier, 4 + experts - 1)

    count = [0]
    sent = []

    def copy_to(src, dst, device):
        number = count[0]
        count[0] += 1
        return pltpu.make_async_remote_copy(
            src_ref=src,
            dst_ref=dst,
            send_sem=send_sem.at[number],
            recv_sem=recv_sem.at[number],
            device_id=device,
            device_id_type=MESH,
        )

    def send(src, dst, device):
        copy = copy_to(src, dst, device)
        copy.start()
        sent.append(copy)
        return copy

    dispatch = {}
    for j in (1, 15, 2, 14, 3, 13, 4, 12, 5, 11, 6, 10, 7, 9, 8):
        peer = {"expert": lax.rem(expert + j, experts)}
        dispatch[j] = send(leaving.at[j], landed.at[j], peer)

    chosen_slot = 0
    for j in range(2 * RING):
        chosen_slot += jnp.where(source_ref[0, j] == dp, hand_slot_ref[0, j], 0)
    cache_load.wait()
    chosen[...] = cache[chosen_slot, ROPE : ROPE + chosen.shape[0], :]
    half = held.shape[2]
    lat = held.shape[1]
    first_cross = copy_to(chosen.at[:, half : 2 * half], held.at[0], other_section)

    @pl.when(section == 0)
    def _():
        first_cross.start()
        held[0] = chosen[:, 0:half]

    def hand_hop(hops):
        if hops < 4:
            ahead = send(held.at[(RING - hops + 1) % RING], held.at[RING - hops], y_next)
            back = send(held.at[hops - 1], held.at[hops], y_back)
        else:
            ahead = send(held.at[RING - 3, 0 : lat // 2], held.at[4, 0 : lat // 2], y_next)
            back = send(held.at[3, lat // 2 : lat], held.at[4, lat // 2 : lat], y_back)
        return ahead, back

    hand = [
        copy_to(held.at[0], held.at[RING - 1], y_next),
        copy_to(held.at[0], held.at[1], y_back),
    ]
    sent.extend(hand)
    first_hop = list(hand)

    @pl.when(section == 0)
    def _():
        for copy in first_hop:
            copy.start()

    order = ((0, 1, 15, 2, 14, 3, 13, 4), (12, 5, 11, 6, 10, 7, 9, 8))
    block = rows.shape[1] // (2 * RING)

    def land(h):
        for i, j in enumerate(order[h]):
            if j == 0:
                rows[h, CAP * i : CAP * (i + 1), :] = picked_rows[0:CAP, :]
            else:
                dispatch[j].wait_recv()
                rows[h, CAP * i : CAP * (i + 1), :] = landed[j]

    def place(ref, h, number, start=0, stop=None):
        stop = width if stop is None else stop
        return ref.at[h, number * block : (number + 1) * block, start:stop]

    def ways_at(hops, h):
        return (0, 1) if hops < 4 else (h,)

    own = {}
    other = {}
    crossing = {}

    def own_hop(h, hops, way):
        own[h, hops, way] = send(
            place(rows, h, slot(0, way, hops - 1)), place(rows, h, slot(0, way, hops)), ways[way]
        )

    def other_hop(h, hops, way):
        other[h, hops, way] = send(
            place(rows, h, slot(1, way, hops - 1), 0, SPLIT),
            place(rows, h, slot(1, way, hops), 0, SPLIT),
            ways[way],
        )

    def cross_hop(h, hops, way):
        start = 0 if hops == 0 else SPLIT
        crossing[h, hops, way] = send(
            place(rows, h, slot(0, way, hops), start),
            place(rows, h, slot(1, way, hops), start),
            across,
        )

    def gather_start(h):
        cross_hop(h, 0, 0)
        for way in (0, 1):
            own_hop(h, 1, way)

    def gather_other(h):
        crossing[h, 0, 0].wait_recv()
        for way in (0, 1):
            other_hop(h, 1, way)

    def gather_step(h, hops):
        for way in ways_at(hops, h):
            own[h, hops, way].wait_recv()
            if hops < 4 and way in ways_at(hops + 1, h):
                own_hop(h, hops + 1, way)
            cross_hop(h, hops, way)
        for way in ways_at(hops, h):
            other[h, hops, way].wait_recv()
            if hops < 4 and way in ways_at(hops + 1, h):
                other_hop(h, hops + 1, way)

    def feed_forward(h, first, last):
        chunk = 512
        acc = jnp.dot(rows[h, first:last, :], gate_up[...], preferred_element_type=jnp.float32)
        gate = acc[:, 0:128]
        hidden = (gate / (1.0 + jnp.exp(-gate)) * acc[:, 128:256]).astype(jnp.bfloat16)
        for start in range(0, width, chunk):
            parts[h, first:last, start : start + chunk] = jnp.dot(
                hidden, down[:, start : start + chunk], preferred_element_type=jnp.float32
            ).astype(jnp.bfloat16)

    def near_experts(h):
        for hops in (1, 2):
            for way in (0, 1):
                crossing[h, hops, way].wait_recv()
        feed_forward(h, 0, 10 * block)

    def far_experts(h):
        for hops in (3, 4):
            for way in ways_at(hops, h):
                crossing[h, hops, way].wait_recv()
        feed_forward(h, 10 * block, 16 * block)

    over_x = {}
    home = {}
    last_cross = {}

    def number_of(hops, way):
        if hops == 0:
            return 0
        if hops == 4:
            return 7
        return 1 + (hops - 1) * 2 + way

    def sum_cross(h, hops, way):
        over_x[h, hops, way] = send(
            place(parts, h, slot(1, way, hops), SPLIT),
            place(from_x, h, number_of(hops, way), 0, width - SPLIT),
            across,
        )

    def take_cross(h, hops, way):
        over_x[h, hops, way].wait_recv()
        add_blocks(h, slot(0, way, hops), SPLIT, width, [(from_x, number_of(hops, way), SPLIT)])

    def sum_hop(h, hops, way, col):
        stop = width if col == 0 else SPLIT
        landing = from_y if col == 0 else from_y_other
        home[h, hops, way, col] = send(
            place(parts, h, slot(col, way, hops), 0, stop),
            place(landing, h, (hops - 1) * 2 + way, 0, stop),
            homeward[way],
        )

    def take_other(h, hops, way):
        home[h, hops, way, 1].wait_recv()
        number = (hops - 1) * 2 + way
        add_blocks(h, slot(1, way, hops - 1), 0, SPLIT, [(from_y_other, number, 0)])

    def add_blocks(h, number, start, stop, terms):
        to_rows = slice(number * block, (number + 1) * block)
        for lo in range(start, stop, 512):
            total = parts[h, to_rows, lo : lo + 512].astype(jnp.float32)
            for ref, ref_number, offset in terms:
                ref_rows = slice(ref_number * block, (ref_number + 1) * block)
                if lo >= offset:
                    total = total + ref[
                        h, ref_rows, lo - offset : lo - offset + 512
                    ].astype(jnp.float32)
            parts[h, to_rows, lo : lo + 512] = total.astype(jnp.bfloat16)

    def sum_start(h):
        for hops in (4, 3, 2, 1):
            for way in ways_at(hops, h)[:: 1 if h else -1]:
                sum_cross(h, hops, way)
        sum_cross(h, 0, 0)
        sum_hop(h, 4, h, 1)
        sum_hop(h, 3, 1 - h, 1)
        take_cross(h, 4, h)
        sum_hop(h, 4, h, 0)
        take_cross(h, 3, 1 - h)
        sum_hop(h, 3, 1 - h, 0)

    def sum_step(h, hops):
        going_on = (0, 1) if hops < 3 else (h,)
        for way in going_on:
            take_other(h, hops + 1, way)
            sum_hop(h, hops, way, 1)
        for way in going_on:
            over_x[h, hops, way].wait_recv()
            home[h, hops + 1, way, 0].wait_recv()
            terms = [(from_y, hops * 2 + way, 0), (from_x, number_of(hops, way), SPLIT)]
            add_blocks(h, slot(0, way, hops), 0, width, terms)
            sum_hop(h, hops, way, 0)

    def sum_end(h):
        for way in (0, 1):
            home[h, 1, way, 1].wait_recv()
        add_blocks(h, 1, 0, SPLIT, [(from_y_other, 0, 0), (from_y_other, 1, 0)])
        last_cross[h] = send(place(parts, h, 1, 0, SPLIT), place(from_x_last, h, 0, 0, SPLIT), across)
        over_x[h, 0, 0].wait_recv()
        for way in (0, 1):
            home[h, 1, way, 0].wait_recv()
        add_blocks(h, 0, 0, width, [(from_y, 0, 0), (from_y, 1, 0), (from_x, 0, SPLIT)])

    steps = new_ref.shape[1]
    fresh_even[...] = jnp.zeros(fresh_even.shape, fresh_even.dtype)
    fresh_odd[...] = jnp.zeros(fresh_odd.shape, fresh_odd.dtype)
    for r in range(fresh_even.shape[0]):
        fresh_even[r, 0:steps, 0:lat] = new_ref[r]
        fresh_odd[r, 0:steps, ROPE : ROPE + lat] = new_ref[r]
    for ref in (cache.at[0], cache.at[1], handed):
        ref[0:ROPE, :] = jnp.zeros((ROPE, 2 * half), jnp.bfloat16)
        ref[ROPE + lat :, :] = jnp.zeros((ROPE, 2 * half), jnp.bfloat16)
    reqs = cache.shape[0]
    kv = lat - ROPE
    window = lat + ROPE
    pairs = query.shape[2] // (2 * lat)
    device = (section * experts + expert) * (2 * RING) + dp
    source = source_ref[0, dp]
    source_across = source_ref[0, (1 - x) * RING + y]

    def attend(r, keys, length):
        for p in range(pairs):
            lo = 2 * lat * p
            even[steps * p : steps * (p + 1), :] = query[r, :, lo : lo + window]
            odd[steps * p : steps * (p + 1), :] = query[r, :, lo + lat - ROPE : lo + 2 * lat]
        over_last = (((1,), (1,)), ((), ()))
        scores = softmax_scale * jnp.concatenate(
            [
                jnp.dot(even[...], keys[ROPE:, :], preferred_element_type=jnp.float32),
                jnp.dot(odd[...], keys[0:window, :], preferred_element_type=jnp.float32),
            ],
            axis=0,
        )
        new_scores = softmax_scale * jnp.concatenate(
            [
                lax.dot_general(
                    queries[...], new[r], over_last, preferred_element_type=jnp.float32
                )
                for queries, new in ((even, fresh_even), (odd, fresh_odd))
            ],
            axis=0,
        )
        lane = lax.broadcasted_iota(jnp.int32, scores.shape, 1)
        new_lane = lax.broadcasted_iota(jnp.int32, new_scores.shape, 1)
        step = lax.rem(lax.broadcasted_iota(jnp.int32, new_scores.shape, 0), steps)
        scores = jnp.where(lane < length, scores, -jnp.inf)
        new_scores = jnp.where(new_lane <= step, new_scores, -jnp.inf)
        top = jnp.maximum(
            jnp.max(scores, axis=1, keepdims=True), jnp.max(new_scores, axis=1, keepdims=True)
        )
        weights = jnp.exp(scores - top)
        new_weights = jnp.exp(new_scores - top)
        total = jnp.sum(weights, axis=1, keepdims=True) + jnp.sum(
            new_weights, axis=1, keepdims=True
        )
        context[...] = (
            lax.dot_general(
                (weights / total).astype(jnp.bfloat16),
                keys[ROPE : ROPE + kv, :],
                over_last,
                preferred_element_type=jnp.float32,
            )
            + jnp.dot(
                (new_weights / total).astype(jnp.bfloat16),
                fresh_even[r, :, 0:kv],
                preferred_element_type=jnp.float32,
            )
        ).astype(jnp.bfloat16)
        for p in range(pairs):
            for parity in (0, 1):
                first = (parity * pairs + p) * steps
                lo = (2 * p + parity) * kv
                context_ref[r, :, lo : lo + kv] = context[first : first + steps, :]

    land(0)
    gather_start(0)
    land(1)
    gather_start(1)
    for load in loads:
        load.wait()
    gather_other(0)
    gather_other(1)

    @pl.when(section == 1)
    def _():
        first_cross.wait_recv()
        for copy in first_hop:
            copy.start()

    for h in (0, 1):
        gather_step(h, 1)
    for arrived in hand:
        arrived.wait_recv()
    hand = hand_hop(2)
    attend(0, cache.at[0], len_ref[device * reqs])
    for h in (0, 1):
        gather_step(h, 2)
    attend(1, cache.at[1], len_ref[device * reqs + 1])
    for h in (0, 1):
        gather_step(h, 3)
        near_experts(h)
    for h in (0, 1):
        gather_step(h, 4)
    for arrived in hand:
        arrived.wait_recv()
    hand = hand_hop(3)
    for h in (0, 1):
        far_experts(h)
        sum_start(h)
    for h in (0, 1):
        sum_step(h, 3)
    for arrived in hand:
        arrived.wait_recv()
    hand = hand_hop(4)
    for h in (0, 1):
        sum_step(h, 2)
    for arrived in hand:
        arrived.wait_recv()
    pick_out[...] = held[lax.rem(lax.rem(source_across, RING) - y + RING, RING)]
    pick_pair[0] = held[lax.rem(lax.rem(source, RING) - y + RING, RING)]
    swap = send(pick_out, pick_pair.at[1], across)
    for h in (0, 1):
        sum_step(h, 1)
    for h in (0, 1):
        sum_end(h)

    swap.wait_recv()
    picked[...] = pick_pair[jnp.where(source // RING == x, 0, 1)]
    second_cross = copy_to(picked, handed_half, other_section)
    handed[ROPE : ROPE + lat, half : 2 * half] = picked[...]

    @pl.when(section == 0)
    def _():
        second_cross.start()
        handed[ROPE : ROPE + lat, 0:half] = picked[...]

    back = {}
    for h in (0, 1):
        last_cross[h].wait_recv()
        add_blocks(h, 0, 0, SPLIT, [(from_x_last, 0, 0)])
        for i, j in enumerate(order[h]):
            if j == 0:
                picked_rows[0:CAP, :] = parts[h, CAP * i : CAP * (i + 1), :]
            else:
                going[j] = parts[h, CAP * i : CAP * (i + 1), :]
                back[j] = send(
                    going.at[j], coming.at[j], {"expert": lax.rem(expert + experts - j, experts)}
                )

    @pl.when(section == 1)
    def _():
        second_cross.wait_recv()
        handed[ROPE : ROPE + lat, 0:half] = handed_half[...]

    source_row = (expert * 2 * RING + source) * reqs + hand_slot_ref[0, dp]
    attend(reqs, handed, jnp.where(section == 1, len_ref[source_row], 0))

    for j in range(1, experts):
        back[j].wait_recv()
        picked_rows[CAP * j : CAP * (j + 1), :] = coming[j]
    moe_ref[...] = lax.dot_general(
        mixing,
        picked_rows[...].astype(jnp.float32),
        (((0,), (0,)), ((), ())),
        precision=highest,
    ).astype(jnp.bfloat16)

    for copy in sent:
        copy.wait_send()

    @pl.when(section == 0)
    def _():
        first_cross.wait_send()
        second_cross.wait_send()


def shards(
    tokens,
    route_ids,
    route_weight,
    gate_weight,
    up_weight,
    down_weight,
    latent_cache,
    cache_len,
    hand_source,
    hand_slot,
    query_latent,
    new_latent,
):
    tok_rows, width = tokens.shape
    experts = lax.axis_size("expert")
    slot_count, step_count, _ = query_latent.shape
    requests, max_len, lat = latent_cache.shape
    lane_rows = experts * CAP
    half = max_len // 2
    kv = lat - ROPE
    query_rows = query_latent.shape[1] * query_latent.shape[2] // lat
    bf16 = jnp.bfloat16
    smem = pl.BlockSpec(memory_space=pltpu.SMEM)
    vmem = pl.BlockSpec(memory_space=pltpu.VMEM)
    anywhere = pl.BlockSpec(memory_space=pl.ANY)
    return pl.pallas_call(
        exchange,
        out_shape=(
            jax.ShapeDtypeStruct((tok_rows, width), bf16),
            jax.ShapeDtypeStruct((slot_count, step_count, query_rows // step_count * kv), bf16),
        ),
        in_specs=[smem] * 3 + [vmem] * 4 + [anywhere] * 5,
        out_specs=(vmem, vmem),
        scratch_shapes=[
            pltpu.VMEM((lane_rows, width), bf16),
            pltpu.VMEM((experts, CAP, width), bf16),
            pltpu.VMEM((experts, CAP, width), bf16),
            pltpu.VMEM((2, 8 * lane_rows, width), bf16),
            pltpu.VMEM((2, 8 * lane_rows, width), bf16),
            pltpu.VMEM((2, 4 * lane_rows, width), bf16),
            pltpu.VMEM((2, 4 * lane_rows, SPLIT), bf16),
            pltpu.VMEM((2, 4 * lane_rows, width - SPLIT), bf16),
            pltpu.VMEM((2, lane_rows // 2, SPLIT), bf16),
            pltpu.VMEM((experts, CAP, width), bf16),
            pltpu.VMEM((experts, CAP, width), bf16),
            pltpu.VMEM((requests, lat + 2 * ROPE, max_len), bf16),
            pltpu.VMEM(query_latent.shape, bf16),
            pltpu.VMEM((slot_count, 16, lat + ROPE), bf16),
            pltpu.VMEM((slot_count, 16, lat + ROPE), bf16),
            pltpu.VMEM((query_rows // 2, lat + ROPE), bf16),
            pltpu.VMEM((query_rows // 2, lat + ROPE), bf16),
            pltpu.VMEM((query_rows, kv), bf16),
            pltpu.VMEM((lat, max_len), bf16),
            pltpu.VMEM((RING, lat, half), bf16),
            pltpu.VMEM((2, lat, half), bf16),
            pltpu.VMEM((lat, half), bf16),
            pltpu.VMEM((lat, half), bf16),
            pltpu.VMEM((lat, half), bf16),
            pltpu.VMEM((lat + 2 * ROPE, max_len), bf16),
            pltpu.VMEM((width, 256), bf16),
            pltpu.VMEM((128, width), bf16),
            pltpu.SemaphoreType.DMA((160,)),
            pltpu.SemaphoreType.DMA((160,)),
            pltpu.SemaphoreType.DMA((5,)),
        ],
        compiler_params=pltpu.CompilerParams(
            collective_id=0, has_side_effects=True, vmem_limit_bytes=62 * 1024 * 1024
        ),
    )(
        hand_source,
        hand_slot,
        cache_len,
        tokens,
        route_ids.T,
        route_weight.T,
        new_latent,
        jnp.swapaxes(latent_cache, 1, 2),
        query_latent,
        gate_weight[0],
        up_weight[0],
        down_weight[0],
    )


def solution(mesh):
    return jax.shard_map(
        shards,
        mesh=mesh,
        in_specs=(
            P(("section", "expert", "dp"), None),
            P(("section", "expert", "dp"), None),
            P(("section", "expert", "dp"), None),
            P(("section", "expert"), None, "dp"),
            P(("section", "expert"), None, "dp"),
            P(("section", "expert"), "dp", None),
            P(("section", "expert", "dp"), None, None),
            P(),
            P("expert", None),
            P("expert", None),
            P(("section", "expert", "dp"), None, None),
            P(("section", "expert", "dp"), None, None),
        ),
        out_specs=(
            P(("section", "expert", "dp"), None),
            P(("section", "expert", "dp"), None, None),
        ),
        check_vma=False,
    )
```

```python
import jax
import jax.numpy as jnp
from jax import lax
from jax.experimental import pallas as pl
from jax.experimental.pallas import tpu as pltpu
from jax.sharding import PartitionSpec as P

CAP = 2
ROPE = 64
RING = 8
SPLIT = 1536
MESH = pl.DeviceIdType.MESH

softmax_scale = 192.0 ** (-0.5)
highest = lax.Precision.HIGHEST


def slot(col, way, hops):
    if hops == 0:
        return col
    if hops == 4:
        return 14 + col
    return 2 + (hops - 1) * 4 + col * 2 + way


def exchange(
    source_ref,
    hand_slot_ref,
    len_ref,
    tokens_ref,
    ids_ref,
    weight_ref,
    new_ref,
    cache_ref,
    query_ref,
    gate_ref,
    up_ref,
    down_ref,
    moe_ref,
    context_ref,
    picked_rows,
    leaving,
    landed,
    rows,
    parts,
    from_y,
    from_y_other,
    from_x,
    from_x_last,
    going,
    coming,
    cache,
    query,
    fresh_even,
    fresh_odd,
    even,
    odd,
    context,
    chosen,
    held,
    pick_pair,
    pick_out,
    picked,
    handed_half,
    handed,
    gate_up,
    down,
    send_sem,
    recv_sem,
    local_sem,
):
    width = rows.shape[2]
    section = lax.axis_index("section")
    expert = lax.axis_index("expert")
    dp = lax.axis_index("dp")
    experts = leaving.shape[0]
    x = dp // RING
    y = lax.rem(dp, RING)
    y_next = {"dp": x * RING + lax.rem(y + 1, RING)}
    y_back = {"dp": x * RING + lax.rem(y + RING - 1, RING)}
    across = {"dp": (1 - x) * RING + y}
    other_section = {"section": 1 - section}
    ways = (y_next, y_back)
    homeward = (y_back, y_next)

    loads = [
        pltpu.make_async_copy(gate_ref, gate_up.at[:, 0:128], local_sem.at[0]),
        pltpu.make_async_copy(up_ref, gate_up.at[:, 128:256], local_sem.at[1]),
        pltpu.make_async_copy(down_ref, down, local_sem.at[2]),
        pltpu.make_async_copy(query_ref, query, local_sem.at[3]),
    ]
    cache_load = pltpu.make_async_copy(
        cache_ref, cache.at[:, ROPE : ROPE + cache_ref.shape[1]], local_sem.at[4]
    )
    cache_load.start()
    for load in loads:
        load.start()

    barrier = pltpu.get_barrier_semaphore()
    for peer in (y_next, y_back, across, other_section):
        pl.semaphore_signal(barrier, inc=1, device_id=peer, device_id_type=MESH)
    for j in range(1, experts):
        peer = {"expert": lax.rem(expert + j, experts)}
        pl.semaphore_signal(barrier, inc=1, device_id=peer, device_id_type=MESH)

    choices, tok_rows = ids_ref.shape
    slots = experts * CAP
    relative = lax.rem(ids_ref[...] - expert + experts, experts)
    slot_row = lax.broadcasted_iota(jnp.int32, (slots, tok_rows), 0)
    hits = jnp.zeros((slots, tok_rows), jnp.float32)
    mixing = jnp.zeros((slots, tok_rows), jnp.float32)
    for k in range(choices):
        hit = relative[k : k + 1, :] == slot_row // CAP
        hits = hits + jnp.where(hit, 1.0, 0.0)
        mixing = mixing + jnp.where(hit, weight_ref[k : k + 1, :], 0.0)
    token_row = lax.broadcasted_iota(jnp.int32, (tok_rows, tok_rows), 0)
    token_lane = lax.broadcasted_iota(jnp.int32, (tok_rows, tok_rows), 1)
    before = jnp.where(token_row < token_lane, 1.0, 0.0)
    earlier = jnp.dot(
        hits.astype(jnp.bfloat16), before.astype(jnp.bfloat16), preferred_element_type=jnp.float32
    )
    taken = jnp.where(earlier == lax.rem(slot_row, CAP).astype(jnp.float32), hits, 0.0)
    mixing = mixing * taken
    picked_rows[...] = jnp.dot(
        taken.astype(jnp.bfloat16), tokens_ref[...], preferred_element_type=jnp.float32
    ).astype(jnp.bfloat16)
    for j in range(1, experts):
        leaving[j] = picked_rows[CAP * j : CAP * (j + 1), :]
    pl.semaphore_wait(barrier, 4 + experts - 1)

    count = [0]
    sent = []

    def copy_to(src, dst, device):
        number = count[0]
        count[0] += 1
        return pltpu.make_async_remote_copy(
            src_ref=src,
            dst_ref=dst,
            send_sem=send_sem.at[number],
            recv_sem=recv_sem.at[number],
            device_id=device,
            device_id_type=MESH,
        )

    def send(src, dst, device):
        copy = copy_to(src, dst, device)
        copy.start()
        sent.append(copy)
        return copy

    dispatch = {}
    for j in (1, 15, 2, 14, 3, 13, 4, 12, 5, 11, 6, 10, 7, 9, 8):
        peer = {"expert": lax.rem(expert + j, experts)}
        dispatch[j] = send(leaving.at[j], landed.at[j], peer)

    chosen_slot = 0
    for j in range(2 * RING):
        chosen_slot += jnp.where(source_ref[0, j] == dp, hand_slot_ref[0, j], 0)
    cache_load.wait()
    chosen[...] = cache[chosen_slot, ROPE : ROPE + chosen.shape[0], :]
    half = held.shape[2]
    lat = held.shape[1]
    first_cross = copy_to(chosen.at[:, half : 2 * half], held.at[0], other_section)

    @pl.when(section == 0)
    def _():
        first_cross.start()
        held[0] = chosen[:, 0:half]

    def hand_hop(hops):
        if hops < 4:
            ahead = send(held.at[(RING - hops + 1) % RING], held.at[RING - hops], y_next)
            back = send(held.at[hops - 1], held.at[hops], y_back)
        else:
            ahead = send(held.at[RING - 3, 0 : lat // 2], held.at[4, 0 : lat // 2], y_next)
            back = send(held.at[3, lat // 2 : lat], held.at[4, lat // 2 : lat], y_back)
        return ahead, back

    hand = [
        copy_to(held.at[0], held.at[RING - 1], y_next),
        copy_to(held.at[0], held.at[1], y_back),
    ]
    sent.extend(hand)
    first_hop = list(hand)

    @pl.when(section == 0)
    def _():
        for copy in first_hop:
            copy.start()

    order = ((0, 1, 15, 2, 14, 3, 13, 4), (12, 5, 11, 6, 10, 7, 9, 8))
    block = rows.shape[1] // (2 * RING)

    def land(h):
        for i, j in enumerate(order[h]):
            if j == 0:
                rows[h, CAP * i : CAP * (i + 1), :] = picked_rows[0:CAP, :]
            else:
                dispatch[j].wait_recv()
                rows[h, CAP * i : CAP * (i + 1), :] = landed[j]

    def place(ref, h, number, start=0, stop=None):
        stop = width if stop is None else stop
        return ref.at[h, number * block : (number + 1) * block, start:stop]

    def ways_at(hops, h):
        return (0, 1) if hops < 4 else (h,)

    own = {}
    other = {}
    crossing = {}

    def own_hop(h, hops, way):
        own[h, hops, way] = send(
            place(rows, h, slot(0, way, hops - 1)), place(rows, h, slot(0, way, hops)), ways[way]
        )

    def other_hop(h, hops, way):
        other[h, hops, way] = send(
            place(rows, h, slot(1, way, hops - 1), 0, SPLIT),
            place(rows, h, slot(1, way, hops), 0, SPLIT),
            ways[way],
        )

    def cross_hop(h, hops, way):
        start = 0 if hops == 0 else SPLIT
        crossing[h, hops, way] = send(
            place(rows, h, slot(0, way, hops), start),
            place(rows, h, slot(1, way, hops), start),
            across,
        )

    def gather_start(h):
        cross_hop(h, 0, 0)
        for way in (0, 1):
            own_hop(h, 1, way)

    def gather_other(h):
        crossing[h, 0, 0].wait_recv()
        for way in (0, 1):
            other_hop(h, 1, way)

    def gather_step(h, hops):
        for way in ways_at(hops, h):
            own[h, hops, way].wait_recv()
            if hops < 4 and way in ways_at(hops + 1, h):
                own_hop(h, hops + 1, way)
            cross_hop(h, hops, way)
        for way in ways_at(hops, h):
            other[h, hops, way].wait_recv()
            if hops < 4 and way in ways_at(hops + 1, h):
                other_hop(h, hops + 1, way)

    def feed_forward(h, first, last):
        chunk = 512
        acc = jnp.dot(rows[h, first:last, :], gate_up[...], preferred_element_type=jnp.float32)
        gate = acc[:, 0:128]
        hidden = (gate / (1.0 + jnp.exp(-gate)) * acc[:, 128:256]).astype(jnp.bfloat16)
        for start in range(0, width, chunk):
            parts[h, first:last, start : start + chunk] = jnp.dot(
                hidden, down[:, start : start + chunk], preferred_element_type=jnp.float32
            ).astype(jnp.bfloat16)

    def near_experts(h):
        for hops in (1, 2):
            for way in (0, 1):
                crossing[h, hops, way].wait_recv()
        feed_forward(h, 0, 10 * block)

    def far_experts(h):
        for hops in (3, 4):
            for way in ways_at(hops, h):
                crossing[h, hops, way].wait_recv()
        feed_forward(h, 10 * block, 16 * block)

    over_x = {}
    home = {}
    last_cross = {}

    def number_of(hops, way):
        if hops == 0:
            return 0
        if hops == 4:
            return 7
        return 1 + (hops - 1) * 2 + way

    def sum_cross(h, hops, way):
        over_x[h, hops, way] = send(
            place(parts, h, slot(1, way, hops), SPLIT),
            place(from_x, h, number_of(hops, way), 0, width - SPLIT),
            across,
        )

    def take_cross(h, hops, way):
        over_x[h, hops, way].wait_recv()
        add_blocks(h, slot(0, way, hops), SPLIT, width, [(from_x, number_of(hops, way), SPLIT)])

    def sum_hop(h, hops, way, col):
        stop = width if col == 0 else SPLIT
        landing = from_y if col == 0 else from_y_other
        home[h, hops, way, col] = send(
            place(parts, h, slot(col, way, hops), 0, stop),
            place(landing, h, (hops - 1) * 2 + way, 0, stop),
            homeward[way],
        )

    def take_other(h, hops, way):
        home[h, hops, way, 1].wait_recv()
        number = (hops - 1) * 2 + way
        add_blocks(h, slot(1, way, hops - 1), 0, SPLIT, [(from_y_other, number, 0)])

    def add_blocks(h, number, start, stop, terms):
        to_rows = slice(number * block, (number + 1) * block)
        for lo in range(start, stop, 512):
            total = parts[h, to_rows, lo : lo + 512].astype(jnp.float32)
            for ref, ref_number, offset in terms:
                ref_rows = slice(ref_number * block, (ref_number + 1) * block)
                if lo >= offset:
                    total = total + ref[
                        h, ref_rows, lo - offset : lo - offset + 512
                    ].astype(jnp.float32)
            parts[h, to_rows, lo : lo + 512] = total.astype(jnp.bfloat16)

    def sum_start(h):
        for hops in (4, 3, 2, 1):
            for way in ways_at(hops, h)[:: 1 if h else -1]:
                sum_cross(h, hops, way)
        sum_cross(h, 0, 0)
        sum_hop(h, 4, h, 1)
        sum_hop(h, 3, 1 - h, 1)
        take_cross(h, 4, h)
        sum_hop(h, 4, h, 0)
        take_cross(h, 3, 1 - h)
        sum_hop(h, 3, 1 - h, 0)

    def sum_step(h, hops):
        going_on = (0, 1) if hops < 3 else (h,)
        for way in going_on:
            take_other(h, hops + 1, way)
            sum_hop(h, hops, way, 1)
        for way in going_on:
            over_x[h, hops, way].wait_recv()
            home[h, hops + 1, way, 0].wait_recv()
            terms = [(from_y, hops * 2 + way, 0), (from_x, number_of(hops, way), SPLIT)]
            add_blocks(h, slot(0, way, hops), 0, width, terms)
            sum_hop(h, hops, way, 0)

    def sum_end(h):
        for way in (0, 1):
            home[h, 1, way, 1].wait_recv()
        add_blocks(h, 1, 0, SPLIT, [(from_y_other, 0, 0), (from_y_other, 1, 0)])
        last_cross[h] = send(place(parts, h, 1, 0, SPLIT), place(from_x_last, h, 0, 0, SPLIT), across)
        over_x[h, 0, 0].wait_recv()
        for way in (0, 1):
            home[h, 1, way, 0].wait_recv()
        add_blocks(h, 0, 0, width, [(from_y, 0, 0), (from_y, 1, 0), (from_x, 0, SPLIT)])

    steps = new_ref.shape[1]
    fresh_even[...] = jnp.zeros(fresh_even.shape, fresh_even.dtype)
    fresh_odd[...] = jnp.zeros(fresh_odd.shape, fresh_odd.dtype)
    for r in range(fresh_even.shape[0]):
        fresh_even[r, 0:steps, 0:lat] = new_ref[r]
        fresh_odd[r, 0:steps, ROPE : ROPE + lat] = new_ref[r]
    for ref in (cache.at[0], cache.at[1], handed):
        ref[0:ROPE, :] = jnp.zeros((ROPE, 2 * half), jnp.bfloat16)
        ref[ROPE + lat :, :] = jnp.zeros((ROPE, 2 * half), jnp.bfloat16)
    reqs = cache.shape[0]
    kv = lat - ROPE
    window = lat + ROPE
    pairs = query.shape[2] // (2 * lat)
    device = (section * experts + expert) * (2 * RING) + dp
    source = source_ref[0, dp]
    source_across = source_ref[0, (1 - x) * RING + y]

    def attend(r, keys, length):
        for p in range(pairs):
            lo = 2 * lat * p
            even[steps * p : steps * (p + 1), :] = query[r, :, lo : lo + window]
            odd[steps * p : steps * (p + 1), :] = query[r, :, lo + lat - ROPE : lo + 2 * lat]
        over_last = (((1,), (1,)), ((), ()))
        scores = softmax_scale * jnp.concatenate(
            [
                jnp.dot(even[...], keys[ROPE:, :], preferred_element_type=jnp.float32),
                jnp.dot(odd[...], keys[0:window, :], preferred_element_type=jnp.float32),
            ],
            axis=0,
        )
        new_scores = softmax_scale * jnp.concatenate(
            [
                lax.dot_general(
                    queries[...], new[r], over_last, preferred_element_type=jnp.float32
                )
                for queries, new in ((even, fresh_even), (odd, fresh_odd))
            ],
            axis=0,
        )
        lane = lax.broadcasted_iota(jnp.int32, scores.shape, 1)
        new_lane = lax.broadcasted_iota(jnp.int32, new_scores.shape, 1)
        step = lax.rem(lax.broadcasted_iota(jnp.int32, new_scores.shape, 0), steps)
        scores = jnp.where(lane < length, scores, -jnp.inf)
        new_scores = jnp.where(new_lane <= step, new_scores, -jnp.inf)
        top = jnp.maximum(
            jnp.max(scores, axis=1, keepdims=True), jnp.max(new_scores, axis=1, keepdims=True)
        )
        weights = jnp.exp(scores - top)
        new_weights = jnp.exp(new_scores - top)
        total = jnp.sum(weights, axis=1, keepdims=True) + jnp.sum(
            new_weights, axis=1, keepdims=True
        )
        context[...] = (
            lax.dot_general(
                (weights / total).astype(jnp.bfloat16),
                keys[ROPE : ROPE + kv, :],
                over_last,
                preferred_element_type=jnp.float32,
            )
            + jnp.dot(
                (new_weights / total).astype(jnp.bfloat16),
                fresh_even[r, :, 0:kv],
                preferred_element_type=jnp.float32,
            )
        ).astype(jnp.bfloat16)
        for p in range(pairs):
            for parity in (0, 1):
                first = (parity * pairs + p) * steps
                lo = (2 * p + parity) * kv
                context_ref[r, :, lo : lo + kv] = context[first : first + steps, :]

    land(0)
    gather_start(0)
    land(1)
    gather_start(1)
    for load in loads:
        load.wait()
    gather_other(0)
    gather_other(1)

    @pl.when(section == 1)
    def _():
        first_cross.wait_recv()
        for copy in first_hop:
            copy.start()

    for h in (0, 1):
        gather_step(h, 1)
    attend(0, cache.at[0], len_ref[device * reqs])
    for h in (0, 1):
        gather_step(h, 2)
    for arrived in hand:
        arrived.wait_recv()
    hand = hand_hop(2)
    attend(1, cache.at[1], len_ref[device * reqs + 1])
    for h in (0, 1):
        gather_step(h, 3)
        near_experts(h)
    for h in (0, 1):
        gather_step(h, 4)
    for arrived in hand:
        arrived.wait_recv()
    hand = hand_hop(3)
    for h in (0, 1):
        far_experts(h)
        sum_start(h)
    for h in (0, 1):
        sum_step(h, 3)
    for arrived in hand:
        arrived.wait_recv()
    hand = hand_hop(4)
    for h in (0, 1):
        sum_step(h, 2)
    for arrived in hand:
        arrived.wait_recv()
    pick_out[...] = held[lax.rem(lax.rem(source_across, RING) - y + RING, RING)]
    pick_pair[0] = held[lax.rem(lax.rem(source, RING) - y + RING, RING)]
    swap = send(pick_out, pick_pair.at[1], across)
    for h in (0, 1):
        sum_step(h, 1)
    for h in (0, 1):
        sum_end(h)

    swap.wait_recv()
    picked[...] = pick_pair[jnp.where(source // RING == x, 0, 1)]
    second_cross = copy_to(picked, handed_half, other_section)
    handed[ROPE : ROPE + lat, half : 2 * half] = picked[...]

    @pl.when(section == 0)
    def _():
        second_cross.start()
        handed[ROPE : ROPE + lat, 0:half] = picked[...]

    back = {}
    for h in (0, 1):
        last_cross[h].wait_recv()
        add_blocks(h, 0, 0, SPLIT, [(from_x_last, 0, 0)])
        for i, j in enumerate(order[h]):
            if j == 0:
                picked_rows[0:CAP, :] = parts[h, CAP * i : CAP * (i + 1), :]
            else:
                going[j] = parts[h, CAP * i : CAP * (i + 1), :]
                back[j] = send(
                    going.at[j], coming.at[j], {"expert": lax.rem(expert + experts - j, experts)}
                )

    @pl.when(section == 1)
    def _():
        second_cross.wait_recv()
        handed[ROPE : ROPE + lat, 0:half] = handed_half[...]

    source_row = (expert * 2 * RING + source) * reqs + hand_slot_ref[0, dp]
    attend(reqs, handed, jnp.where(section == 1, len_ref[source_row], 0))

    for j in range(1, experts):
        back[j].wait_recv()
        picked_rows[CAP * j : CAP * (j + 1), :] = coming[j]
    moe_ref[...] = lax.dot_general(
        mixing,
        picked_rows[...].astype(jnp.float32),
        (((0,), (0,)), ((), ())),
        precision=highest,
    ).astype(jnp.bfloat16)

    for copy in sent:
        copy.wait_send()

    @pl.when(section == 0)
    def _():
        first_cross.wait_send()
        second_cross.wait_send()


def shards(
    tokens,
    route_ids,
    route_weight,
    gate_weight,
    up_weight,
    down_weight,
    latent_cache,
    cache_len,
    hand_source,
    hand_slot,
    query_latent,
    new_latent,
):
    tok_rows, width = tokens.shape
    experts = lax.axis_size("expert")
    slot_count, step_count, _ = query_latent.shape
    requests, max_len, lat = latent_cache.shape
    lane_rows = experts * CAP
    half = max_len // 2
    kv = lat - ROPE
    query_rows = query_latent.shape[1] * query_latent.shape[2] // lat
    bf16 = jnp.bfloat16
    smem = pl.BlockSpec(memory_space=pltpu.SMEM)
    vmem = pl.BlockSpec(memory_space=pltpu.VMEM)
    anywhere = pl.BlockSpec(memory_space=pl.ANY)
    return pl.pallas_call(
        exchange,
        out_shape=(
            jax.ShapeDtypeStruct((tok_rows, width), bf16),
            jax.ShapeDtypeStruct((slot_count, step_count, query_rows // step_count * kv), bf16),
        ),
        in_specs=[smem] * 3 + [vmem] * 4 + [anywhere] * 5,
        out_specs=(vmem, vmem),
        scratch_shapes=[
            pltpu.VMEM((lane_rows, width), bf16),
            pltpu.VMEM((experts, CAP, width), bf16),
            pltpu.VMEM((experts, CAP, width), bf16),
            pltpu.VMEM((2, 8 * lane_rows, width), bf16),
            pltpu.VMEM((2, 8 * lane_rows, width), bf16),
            pltpu.VMEM((2, 4 * lane_rows, width), bf16),
            pltpu.VMEM((2, 4 * lane_rows, SPLIT), bf16),
            pltpu.VMEM((2, 4 * lane_rows, width - SPLIT), bf16),
            pltpu.VMEM((2, lane_rows // 2, SPLIT), bf16),
            pltpu.VMEM((experts, CAP, width), bf16),
            pltpu.VMEM((experts, CAP, width), bf16),
            pltpu.VMEM((requests, lat + 2 * ROPE, max_len), bf16),
            pltpu.VMEM(query_latent.shape, bf16),
            pltpu.VMEM((slot_count, 16, lat + ROPE), bf16),
            pltpu.VMEM((slot_count, 16, lat + ROPE), bf16),
            pltpu.VMEM((query_rows // 2, lat + ROPE), bf16),
            pltpu.VMEM((query_rows // 2, lat + ROPE), bf16),
            pltpu.VMEM((query_rows, kv), bf16),
            pltpu.VMEM((lat, max_len), bf16),
            pltpu.VMEM((RING, lat, half), bf16),
            pltpu.VMEM((2, lat, half), bf16),
            pltpu.VMEM((lat, half), bf16),
            pltpu.VMEM((lat, half), bf16),
            pltpu.VMEM((lat, half), bf16),
            pltpu.VMEM((lat + 2 * ROPE, max_len), bf16),
            pltpu.VMEM((width, 256), bf16),
            pltpu.VMEM((128, width), bf16),
            pltpu.SemaphoreType.DMA((160,)),
            pltpu.SemaphoreType.DMA((160,)),
            pltpu.SemaphoreType.DMA((5,)),
        ],
        compiler_params=pltpu.CompilerParams(
            collective_id=0, has_side_effects=True, vmem_limit_bytes=62 * 1024 * 1024
        ),
    )(
        hand_source,
        hand_slot,
        cache_len,
        tokens,
        route_ids.T,
        route_weight.T,
        new_latent,
        jnp.swapaxes(latent_cache, 1, 2),
        query_latent,
        gate_weight[0],
        up_weight[0],
        down_weight[0],
    )


def solution(mesh):
    return jax.shard_map(
        shards,
        mesh=mesh,
        in_specs=(
            P(("section", "expert", "dp"), None),
            P(("section", "expert", "dp"), None),
            P(("section", "expert", "dp"), None),
            P(("section", "expert"), None, "dp"),
            P(("section", "expert"), None, "dp"),
            P(("section", "expert"), "dp", None),
            P(("section", "expert", "dp"), None, None),
            P(),
            P("expert", None),
            P("expert", None),
            P(("section", "expert", "dp"), None, None),
            P(("section", "expert", "dp"), None, None),
        ),
        out_specs=(
            P(("section", "expert", "dp"), None),
            P(("section", "expert", "dp"), None, None),
        ),
        check_vma=False,
    )
```

```python
import jax
import jax.numpy as jnp
from jax import lax
from jax.experimental import pallas as pl
from jax.experimental.pallas import tpu as pltpu
from jax.sharding import PartitionSpec as P

CAP = 2
ROPE = 64
RING = 8
SPLIT = 1536
MESH = pl.DeviceIdType.MESH

softmax_scale = 192.0 ** (-0.5)
highest = lax.Precision.HIGHEST


def slot(col, way, hops):
    if hops == 0:
        return col
    if hops == 4:
        return 14 + col
    return 2 + (hops - 1) * 4 + col * 2 + way


def exchange(
    source_ref,
    hand_slot_ref,
    len_ref,
    tokens_ref,
    ids_ref,
    weight_ref,
    new_ref,
    cache_ref,
    query_ref,
    gate_ref,
    up_ref,
    down_ref,
    moe_ref,
    context_ref,
    picked_rows,
    leaving,
    landed,
    rows,
    parts,
    from_y,
    from_y_other,
    from_x,
    from_x_last,
    going,
    coming,
    cache,
    query,
    fresh_even,
    fresh_odd,
    even,
    odd,
    context,
    chosen,
    held,
    pick_pair,
    pick_out,
    picked,
    handed_half,
    handed,
    gate_up,
    down,
    send_sem,
    recv_sem,
    local_sem,
):
    width = rows.shape[2]
    section = lax.axis_index("section")
    expert = lax.axis_index("expert")
    dp = lax.axis_index("dp")
    experts = leaving.shape[0]
    x = dp // RING
    y = lax.rem(dp, RING)
    y_next = {"dp": x * RING + lax.rem(y + 1, RING)}
    y_back = {"dp": x * RING + lax.rem(y + RING - 1, RING)}
    across = {"dp": (1 - x) * RING + y}
    other_section = {"section": 1 - section}
    ways = (y_next, y_back)
    homeward = (y_back, y_next)

    loads = [
        pltpu.make_async_copy(gate_ref, gate_up.at[:, 0:128], local_sem.at[0]),
        pltpu.make_async_copy(up_ref, gate_up.at[:, 128:256], local_sem.at[1]),
        pltpu.make_async_copy(down_ref, down, local_sem.at[2]),
        pltpu.make_async_copy(query_ref, query, local_sem.at[3]),
    ]
    cache_load = pltpu.make_async_copy(
        cache_ref, cache.at[:, ROPE : ROPE + cache_ref.shape[1]], local_sem.at[4]
    )
    cache_load.start()
    for load in loads:
        load.start()

    barrier = pltpu.get_barrier_semaphore()
    for peer in (y_next, y_back, across, other_section):
        pl.semaphore_signal(barrier, inc=1, device_id=peer, device_id_type=MESH)
    for j in range(1, experts):
        peer = {"expert": lax.rem(expert + j, experts)}
        pl.semaphore_signal(barrier, inc=1, device_id=peer, device_id_type=MESH)

    choices, tok_rows = ids_ref.shape
    slots = experts * CAP
    relative = lax.rem(ids_ref[...] - expert + experts, experts)
    slot_row = lax.broadcasted_iota(jnp.int32, (slots, tok_rows), 0)
    hits = jnp.zeros((slots, tok_rows), jnp.float32)
    mixing = jnp.zeros((slots, tok_rows), jnp.float32)
    for k in range(choices):
        hit = relative[k : k + 1, :] == slot_row // CAP
        hits = hits + jnp.where(hit, 1.0, 0.0)
        mixing = mixing + jnp.where(hit, weight_ref[k : k + 1, :], 0.0)
    token_row = lax.broadcasted_iota(jnp.int32, (tok_rows, tok_rows), 0)
    token_lane = lax.broadcasted_iota(jnp.int32, (tok_rows, tok_rows), 1)
    before = jnp.where(token_row < token_lane, 1.0, 0.0)
    earlier = jnp.dot(
        hits.astype(jnp.bfloat16), before.astype(jnp.bfloat16), preferred_element_type=jnp.float32
    )
    taken = jnp.where(earlier == lax.rem(slot_row, CAP).astype(jnp.float32), hits, 0.0)
    mixing = mixing * taken
    picked_rows[...] = jnp.dot(
        taken.astype(jnp.bfloat16), tokens_ref[...], preferred_element_type=jnp.float32
    ).astype(jnp.bfloat16)
    for j in range(1, experts):
        leaving[j] = picked_rows[CAP * j : CAP * (j + 1), :]
    pl.semaphore_wait(barrier, 4 + experts - 1)

    count = [0]
    sent = []

    def copy_to(src, dst, device):
        number = count[0]
        count[0] += 1
        return pltpu.make_async_remote_copy(
            src_ref=src,
            dst_ref=dst,
            send_sem=send_sem.at[number],
            recv_sem=recv_sem.at[number],
            device_id=device,
            device_id_type=MESH,
        )

    def send(src, dst, device):
        copy = copy_to(src, dst, device)
        copy.start()
        sent.append(copy)
        return copy

    dispatch = {}
    for j in (1, 15, 2, 14, 3, 13, 4, 12, 5, 11, 6, 10, 7, 9, 8):
        peer = {"expert": lax.rem(expert + j, experts)}
        dispatch[j] = send(leaving.at[j], landed.at[j], peer)

    chosen_slot = 0
    for j in range(2 * RING):
        chosen_slot += jnp.where(source_ref[0, j] == dp, hand_slot_ref[0, j], 0)
    cache_load.wait()
    chosen[...] = cache[chosen_slot, ROPE : ROPE + chosen.shape[0], :]
    half = held.shape[2]
    lat = held.shape[1]
    first_cross = copy_to(chosen.at[:, half : 2 * half], held.at[0], other_section)

    @pl.when(section == 0)
    def _():
        first_cross.start()
        held[0] = chosen[:, 0:half]

    def hand_hop(hops):
        if hops < 4:
            ahead = send(held.at[(RING - hops + 1) % RING], held.at[RING - hops], y_next)
            back = send(held.at[hops - 1], held.at[hops], y_back)
        else:
            ahead = send(held.at[RING - 3, 0 : lat // 2], held.at[4, 0 : lat // 2], y_next)
            back = send(held.at[3, lat // 2 : lat], held.at[4, lat // 2 : lat], y_back)
        return ahead, back

    hand = [
        copy_to(held.at[0], held.at[RING - 1], y_next),
        copy_to(held.at[0], held.at[1], y_back),
    ]
    sent.extend(hand)
    first_hop = list(hand)

    @pl.when(section == 0)
    def _():
        for copy in first_hop:
            copy.start()

    order = ((0, 1, 15, 2, 14, 3, 13, 4), (12, 5, 11, 6, 10, 7, 9, 8))
    block = rows.shape[1] // (2 * RING)

    def land(h):
        for i, j in enumerate(order[h]):
            if j == 0:
                rows[h, CAP * i : CAP * (i + 1), :] = picked_rows[0:CAP, :]
            else:
                dispatch[j].wait_recv()
                rows[h, CAP * i : CAP * (i + 1), :] = landed[j]

    def place(ref, h, number, start=0, stop=None):
        stop = width if stop is None else stop
        return ref.at[h, number * block : (number + 1) * block, start:stop]

    def ways_at(hops, h):
        return (0, 1) if hops < 4 else (h,)

    own = {}
    other = {}
    crossing = {}

    def own_hop(h, hops, way):
        own[h, hops, way] = send(
            place(rows, h, slot(0, way, hops - 1)), place(rows, h, slot(0, way, hops)), ways[way]
        )

    def other_hop(h, hops, way):
        other[h, hops, way] = send(
            place(rows, h, slot(1, way, hops - 1), 0, SPLIT),
            place(rows, h, slot(1, way, hops), 0, SPLIT),
            ways[way],
        )

    def cross_hop(h, hops, way):
        start = 0 if hops == 0 else SPLIT
        crossing[h, hops, way] = send(
            place(rows, h, slot(0, way, hops), start),
            place(rows, h, slot(1, way, hops), start),
            across,
        )

    def gather_start(h):
        cross_hop(h, 0, 0)
        for way in (0, 1):
            own_hop(h, 1, way)

    def gather_other(h):
        crossing[h, 0, 0].wait_recv()
        for way in (0, 1):
            other_hop(h, 1, way)

    def gather_step(h, hops):
        for way in ways_at(hops, h):
            own[h, hops, way].wait_recv()
            if hops < 4 and way in ways_at(hops + 1, h):
                own_hop(h, hops + 1, way)
            cross_hop(h, hops, way)
        for way in ways_at(hops, h):
            other[h, hops, way].wait_recv()
            if hops < 4 and way in ways_at(hops + 1, h):
                other_hop(h, hops + 1, way)

    def feed_forward(h, first, last):
        chunk = 512
        acc = jnp.dot(rows[h, first:last, :], gate_up[...], preferred_element_type=jnp.float32)
        gate = acc[:, 0:128]
        hidden = (gate / (1.0 + jnp.exp(-gate)) * acc[:, 128:256]).astype(jnp.bfloat16)
        for start in range(0, width, chunk):
            parts[h, first:last, start : start + chunk] = jnp.dot(
                hidden, down[:, start : start + chunk], preferred_element_type=jnp.float32
            ).astype(jnp.bfloat16)

    def near_experts(h):
        for hops in (1, 2):
            for way in (0, 1):
                crossing[h, hops, way].wait_recv()
        feed_forward(h, 0, 10 * block)

    def far_experts(h):
        for hops in (3, 4):
            for way in ways_at(hops, h):
                crossing[h, hops, way].wait_recv()
        feed_forward(h, 10 * block, 16 * block)

    over_x = {}
    home = {}
    last_cross = {}

    def number_of(hops, way):
        if hops == 0:
            return 0
        if hops == 4:
            return 7
        return 1 + (hops - 1) * 2 + way

    def sum_cross(h, hops, way):
        over_x[h, hops, way] = send(
            place(parts, h, slot(1, way, hops), SPLIT),
            place(from_x, h, number_of(hops, way), 0, width - SPLIT),
            across,
        )

    def take_cross(h, hops, way):
        over_x[h, hops, way].wait_recv()
        add_blocks(h, slot(0, way, hops), SPLIT, width, [(from_x, number_of(hops, way), SPLIT)])

    def sum_hop(h, hops, way, col):
        stop = width if col == 0 else SPLIT
        landing = from_y if col == 0 else from_y_other
        home[h, hops, way, col] = send(
            place(parts, h, slot(col, way, hops), 0, stop),
            place(landing, h, (hops - 1) * 2 + way, 0, stop),
            homeward[way],
        )

    def take_other(h, hops, way):
        home[h, hops, way, 1].wait_recv()
        number = (hops - 1) * 2 + way
        add_blocks(h, slot(1, way, hops - 1), 0, SPLIT, [(from_y_other, number, 0)])

    def add_blocks(h, number, start, stop, terms):
        to_rows = slice(number * block, (number + 1) * block)
        for lo in range(start, stop, 512):
            total = parts[h, to_rows, lo : lo + 512].astype(jnp.float32)
            for ref, ref_number, offset in terms:
                ref_rows = slice(ref_number * block, (ref_number + 1) * block)
                if lo >= offset:
                    total = total + ref[
                        h, ref_rows, lo - offset : lo - offset + 512
                    ].astype(jnp.float32)
            parts[h, to_rows, lo : lo + 512] = total.astype(jnp.bfloat16)

    def sum_start(h):
        for hops in (4, 3, 2):
            for way in ways_at(hops, h)[:: 1 if h else -1]:
                sum_cross(h, hops, way)
        sum_hop(h, 4, h, 1)
        sum_hop(h, 3, 1 - h, 1)
        take_cross(h, 4, h)
        sum_hop(h, 4, h, 0)
        take_cross(h, 3, 1 - h)
        sum_hop(h, 3, 1 - h, 0)

    def sum_step(h, hops):
        if hops == 3:
            for way in (0, 1):
                sum_cross(h, 1, way)
            sum_cross(h, 0, 0)
        going_on = (0, 1) if hops < 3 else (h,)
        for way in going_on:
            take_other(h, hops + 1, way)
            sum_hop(h, hops, way, 1)
        for way in going_on:
            over_x[h, hops, way].wait_recv()
            home[h, hops + 1, way, 0].wait_recv()
            terms = [(from_y, hops * 2 + way, 0), (from_x, number_of(hops, way), SPLIT)]
            add_blocks(h, slot(0, way, hops), 0, width, terms)
            sum_hop(h, hops, way, 0)

    def sum_end(h):
        for way in (0, 1):
            home[h, 1, way, 1].wait_recv()
        add_blocks(h, 1, 0, SPLIT, [(from_y_other, 0, 0), (from_y_other, 1, 0)])
        last_cross[h] = send(place(parts, h, 1, 0, SPLIT), place(from_x_last, h, 0, 0, SPLIT), across)
        over_x[h, 0, 0].wait_recv()
        for way in (0, 1):
            home[h, 1, way, 0].wait_recv()
        add_blocks(h, 0, 0, width, [(from_y, 0, 0), (from_y, 1, 0), (from_x, 0, SPLIT)])

    steps = new_ref.shape[1]
    fresh_even[...] = jnp.zeros(fresh_even.shape, fresh_even.dtype)
    fresh_odd[...] = jnp.zeros(fresh_odd.shape, fresh_odd.dtype)
    for r in range(fresh_even.shape[0]):
        fresh_even[r, 0:steps, 0:lat] = new_ref[r]
        fresh_odd[r, 0:steps, ROPE : ROPE + lat] = new_ref[r]
    for ref in (cache.at[0], cache.at[1], handed):
        ref[0:ROPE, :] = jnp.zeros((ROPE, 2 * half), jnp.bfloat16)
        ref[ROPE + lat :, :] = jnp.zeros((ROPE, 2 * half), jnp.bfloat16)
    reqs = cache.shape[0]
    kv = lat - ROPE
    window = lat + ROPE
    pairs = query.shape[2] // (2 * lat)
    device = (section * experts + expert) * (2 * RING) + dp
    source = source_ref[0, dp]
    source_across = source_ref[0, (1 - x) * RING + y]

    def attend(r, keys, length):
        for p in range(pairs):
            lo = 2 * lat * p
            even[steps * p : steps * (p + 1), :] = query[r, :, lo : lo + window]
            odd[steps * p : steps * (p + 1), :] = query[r, :, lo + lat - ROPE : lo + 2 * lat]
        over_last = (((1,), (1,)), ((), ()))
        scores = softmax_scale * jnp.concatenate(
            [
                jnp.dot(even[...], keys[ROPE:, :], preferred_element_type=jnp.float32),
                jnp.dot(odd[...], keys[0:window, :], preferred_element_type=jnp.float32),
            ],
            axis=0,
        )
        new_scores = softmax_scale * jnp.concatenate(
            [
                lax.dot_general(
                    queries[...], new[r], over_last, preferred_element_type=jnp.float32
                )
                for queries, new in ((even, fresh_even), (odd, fresh_odd))
            ],
            axis=0,
        )
        lane = lax.broadcasted_iota(jnp.int32, scores.shape, 1)
        new_lane = lax.broadcasted_iota(jnp.int32, new_scores.shape, 1)
        step = lax.rem(lax.broadcasted_iota(jnp.int32, new_scores.shape, 0), steps)
        scores = jnp.where(lane < length, scores, -jnp.inf)
        new_scores = jnp.where(new_lane <= step, new_scores, -jnp.inf)
        top = jnp.maximum(
            jnp.max(scores, axis=1, keepdims=True), jnp.max(new_scores, axis=1, keepdims=True)
        )
        weights = jnp.exp(scores - top)
        new_weights = jnp.exp(new_scores - top)
        total = jnp.sum(weights, axis=1, keepdims=True) + jnp.sum(
            new_weights, axis=1, keepdims=True
        )
        context[...] = (
            lax.dot_general(
                (weights / total).astype(jnp.bfloat16),
                keys[ROPE : ROPE + kv, :],
                over_last,
                preferred_element_type=jnp.float32,
            )
            + jnp.dot(
                (new_weights / total).astype(jnp.bfloat16),
                fresh_even[r, :, 0:kv],
                preferred_element_type=jnp.float32,
            )
        ).astype(jnp.bfloat16)
        for p in range(pairs):
            for parity in (0, 1):
                first = (parity * pairs + p) * steps
                lo = (2 * p + parity) * kv
                context_ref[r, :, lo : lo + kv] = context[first : first + steps, :]

    land(0)
    gather_start(0)
    land(1)
    gather_start(1)
    for load in loads:
        load.wait()
    gather_other(0)
    gather_other(1)

    @pl.when(section == 1)
    def _():
        first_cross.wait_recv()
        for copy in first_hop:
            copy.start()

    for h in (0, 1):
        gather_step(h, 1)
    attend(0, cache.at[0], len_ref[device * reqs])
    for h in (0, 1):
        gather_step(h, 2)
    for arrived in hand:
        arrived.wait_recv()
    hand = hand_hop(2)
    attend(1, cache.at[1], len_ref[device * reqs + 1])
    for h in (0, 1):
        gather_step(h, 3)
        near_experts(h)
    for arrived in hand:
        arrived.wait_recv()
    hand = hand_hop(3)
    for h in (0, 1):
        gather_step(h, 4)
    far_experts(0)
    sum_start(0)
    for arrived in hand:
        arrived.wait_recv()
    hand = hand_hop(4)
    far_experts(1)
    sum_start(1)
    for arrived in hand:
        arrived.wait_recv()
    pick_out[...] = held[lax.rem(lax.rem(source_across, RING) - y + RING, RING)]
    swap = send(pick_out, pick_pair.at[1], across)
    pick_pair[0] = held[lax.rem(lax.rem(source, RING) - y + RING, RING)]
    for hops in (3, 2):
        for h in (0, 1):
            sum_step(h, hops)
    swap.wait_recv()
    picked[...] = pick_pair[jnp.where(source // RING == x, 0, 1)]
    second_cross = copy_to(picked, handed_half, other_section)
    handed[ROPE : ROPE + lat, half : 2 * half] = picked[...]

    @pl.when(section == 0)
    def _():
        second_cross.start()
        handed[ROPE : ROPE + lat, 0:half] = picked[...]

    for h in (0, 1):
        sum_step(h, 1)
    for h in (0, 1):
        sum_end(h)

    back = {}
    for h in (0, 1):
        last_cross[h].wait_recv()
        add_blocks(h, 0, 0, SPLIT, [(from_x_last, 0, 0)])
        for i, j in enumerate(order[h]):
            if j == 0:
                picked_rows[0:CAP, :] = parts[h, CAP * i : CAP * (i + 1), :]
            else:
                going[j] = parts[h, CAP * i : CAP * (i + 1), :]
                back[j] = send(
                    going.at[j], coming.at[j], {"expert": lax.rem(expert + experts - j, experts)}
                )

    @pl.when(section == 1)
    def _():
        second_cross.wait_recv()
        handed[ROPE : ROPE + lat, 0:half] = handed_half[...]

    source_row = (expert * 2 * RING + source) * reqs + hand_slot_ref[0, dp]
    attend(reqs, handed, jnp.where(section == 1, len_ref[source_row], 0))

    for j in range(1, experts):
        back[j].wait_recv()
        picked_rows[CAP * j : CAP * (j + 1), :] = coming[j]
    moe_ref[...] = lax.dot_general(
        mixing,
        picked_rows[...].astype(jnp.float32),
        (((0,), (0,)), ((), ())),
        precision=highest,
    ).astype(jnp.bfloat16)

    for copy in sent:
        copy.wait_send()

    @pl.when(section == 0)
    def _():
        first_cross.wait_send()
        second_cross.wait_send()


def shards(
    tokens,
    route_ids,
    route_weight,
    gate_weight,
    up_weight,
    down_weight,
    latent_cache,
    cache_len,
    hand_source,
    hand_slot,
    query_latent,
    new_latent,
):
    tok_rows, width = tokens.shape
    experts = lax.axis_size("expert")
    slot_count, step_count, _ = query_latent.shape
    requests, max_len, lat = latent_cache.shape
    lane_rows = experts * CAP
    half = max_len // 2
    kv = lat - ROPE
    query_rows = query_latent.shape[1] * query_latent.shape[2] // lat
    bf16 = jnp.bfloat16
    smem = pl.BlockSpec(memory_space=pltpu.SMEM)
    vmem = pl.BlockSpec(memory_space=pltpu.VMEM)
    anywhere = pl.BlockSpec(memory_space=pl.ANY)
    return pl.pallas_call(
        exchange,
        out_shape=(
            jax.ShapeDtypeStruct((tok_rows, width), bf16),
            jax.ShapeDtypeStruct((slot_count, step_count, query_rows // step_count * kv), bf16),
        ),
        in_specs=[smem] * 3 + [vmem] * 4 + [anywhere] * 5,
        out_specs=(vmem, vmem),
        scratch_shapes=[
            pltpu.VMEM((lane_rows, width), bf16),
            pltpu.VMEM((experts, CAP, width), bf16),
            pltpu.VMEM((experts, CAP, width), bf16),
            pltpu.VMEM((2, 8 * lane_rows, width), bf16),
            pltpu.VMEM((2, 8 * lane_rows, width), bf16),
            pltpu.VMEM((2, 4 * lane_rows, width), bf16),
            pltpu.VMEM((2, 4 * lane_rows, SPLIT), bf16),
            pltpu.VMEM((2, 4 * lane_rows, width - SPLIT), bf16),
            pltpu.VMEM((2, lane_rows // 2, SPLIT), bf16),
            pltpu.VMEM((experts, CAP, width), bf16),
            pltpu.VMEM((experts, CAP, width), bf16),
            pltpu.VMEM((requests, lat + 2 * ROPE, max_len), bf16),
            pltpu.VMEM(query_latent.shape, bf16),
            pltpu.VMEM((slot_count, 16, lat + ROPE), bf16),
            pltpu.VMEM((slot_count, 16, lat + ROPE), bf16),
            pltpu.VMEM((query_rows // 2, lat + ROPE), bf16),
            pltpu.VMEM((query_rows // 2, lat + ROPE), bf16),
            pltpu.VMEM((query_rows, kv), bf16),
            pltpu.VMEM((lat, max_len), bf16),
            pltpu.VMEM((RING, lat, half), bf16),
            pltpu.VMEM((2, lat, half), bf16),
            pltpu.VMEM((lat, half), bf16),
            pltpu.VMEM((lat, half), bf16),
            pltpu.VMEM((lat, half), bf16),
            pltpu.VMEM((lat + 2 * ROPE, max_len), bf16),
            pltpu.VMEM((width, 256), bf16),
            pltpu.VMEM((128, width), bf16),
            pltpu.SemaphoreType.DMA((160,)),
            pltpu.SemaphoreType.DMA((160,)),
            pltpu.SemaphoreType.DMA((5,)),
        ],
        compiler_params=pltpu.CompilerParams(
            collective_id=0, has_side_effects=True, vmem_limit_bytes=62 * 1024 * 1024
        ),
    )(
        hand_source,
        hand_slot,
        cache_len,
        tokens,
        route_ids.T,
        route_weight.T,
        new_latent,
        jnp.swapaxes(latent_cache, 1, 2),
        query_latent,
        gate_weight[0],
        up_weight[0],
        down_weight[0],
    )


def solution(mesh):
    return jax.shard_map(
        shards,
        mesh=mesh,
        in_specs=(
            P(("section", "expert", "dp"), None),
            P(("section", "expert", "dp"), None),
            P(("section", "expert", "dp"), None),
            P(("section", "expert"), None, "dp"),
            P(("section", "expert"), None, "dp"),
            P(("section", "expert"), "dp", None),
            P(("section", "expert", "dp"), None, None),
            P(),
            P("expert", None),
            P("expert", None),
            P(("section", "expert", "dp"), None, None),
            P(("section", "expert", "dp"), None, None),
        ),
        out_specs=(
            P(("section", "expert", "dp"), None),
            P(("section", "expert", "dp"), None, None),
        ),
        check_vma=False,
    )
```
